512 devices in a mesh: segment: 2 (over core), dp: 4 (over y), ep: 64 (over z, x).
Axes of the slice: x: 4, y: 4, z: 16, core: 2. Of those that a mesh axis runs over, the one named last changes fastest.
Arguments:
- cache_values: bfloat16 [2, 4, 2, 8192, 512], P('segment', 'dp', None, 'ep'), may hold values from -8 to 8
- cache_rope: bfloat16 [2, 4, 2, 64, 8192], P('segment', 'dp', None, None, 'ep'), may hold values from -6 to 6
- cache_scales: bfloat16 [2, 4, 2, 4, 8192], P('segment', 'dp', None, None, 'ep'), may hold values from 0.29882812 to 3
- queries: bfloat16 [2, 4, 2, 576, 256], P('segment', 'dp'), may hold values from -40 to 40
- new_keys: bfloat16 [2, 4, 2, 2, 576], P('segment', 'dp'), may hold values from -16 to 16
- hidden_rows: bfloat16 [2, 4, 2, 2, 3584], P('segment', 'dp'), may hold values from -6 to 6
- expert_ids: int32 [2, 4, 2, 2, 8], P('segment', 'dp'), may hold values from 0 to 127, all different within a row
- expert_gates: bfloat16 [2, 4, 2, 2, 8], P('segment', 'dp'), may hold values from 0.099609375 to 1
- owners: int32 [2, 4, 2], P('segment', 'dp'), may hold values from 0 to 3, as said below
- lengths: int32 [2, 4, 2], P('segment', 'dp'), may hold values from 1 to 8192, as said below
- up_weight: bfloat16 [128, 3584, 1024], P('ep', None, ('segment', 'dp')), may hold values from -0.09375 to 0.09375
- down_weight: bfloat16 [128, 1024, 3584], P('ep', ('segment', 'dp')), may hold values from -0.1875 to 0.1875
Outputs:
- attention: bfloat16 [2, 4, 4, 2, 128, 512], P('segment', 'dp', None, None, 'ep')
- expert_mix: bfloat16 [2, 4, 4, 2, 3584], P('segment', 'dp')
The draws below stay inside these ranges and needn't reach their ends.
Inputs may be any that keep to these rules, and one draw needn't show every extreme that they name: The requests of one prefill group have different owners; in each section some owner receives a request from every prefill group. `lengths`: in each section some request has the full 8192 positions.
All inputs are finite; a program needn't handle non-finite values.
Results may differ from the reference program's by a relative error of at most 0.0075.
Values may be sent and summed in bfloat16 or wider, within the bound.
A program may use at most 64 MiB of HBM per device.

```python
import math
import jax
import jax.numpy as jnp
from jax import lax

H = 128
LAT = 512
ROPE = 64
QKD = 576
SCALES = 4
D = 3584
FF = 1024
EXP_DEV = 2
TOPK = 8
NEWP = 2
REQ_PRE = 2
CTX_DEV = 128
CTX = 8192
N_SEGMENT = 2
N_DP = 4
N_EP = 64


def latent_base(key):
    return jax.random.normal(key, (N_SEGMENT, N_DP, REQ_PRE, CTX, LAT), jnp.float32)


def draw_cache_values(key, part):
    base = latent_base(key)
    return jnp.clip(base, -6.0, 6.0).astype(jnp.bfloat16)


def draw_queries(key, part):
    key = jax.random.fold_in(key, 12)
    first_key = jax.random.fold_in(key, 0)
    shape = (N_SEGMENT, N_DP, REQ_PRE, QKD, NEWP * H)
    query_cols = jax.random.normal(first_key, shape, jnp.float32) * 0.6
    return jnp.clip(query_cols, -40.0, 40.0).astype(jnp.bfloat16)


def draw_lengths(key, part):
    key = jax.random.fold_in(key, 13)
    first_key, second_key, third_key = jax.random.split(key, 3)
    drawn = jax.random.randint(first_key, (N_SEGMENT, N_DP, REQ_PRE), 1, CTX + 1)
    group_pick = jax.random.randint(second_key, (N_SEGMENT, 1, 1), 0, N_DP)
    request_pick = jax.random.randint(third_key, (N_SEGMENT, 1, 1), 0, REQ_PRE)
    group_iota = jnp.arange(N_DP, dtype=jnp.int32)[None, :, None]
    request_iota = jnp.arange(REQ_PRE, dtype=jnp.int32)[None, None, :]
    longest = (group_iota == group_pick) & (request_iota == request_pick)
    return jnp.where(longest, CTX, drawn).astype(jnp.int32)


def draw_owners(key, part):
    key = jax.random.fold_in(key, 24)
    heavy_key, order_key, slot_key = jax.random.split(key, 3)
    heavy = jax.random.randint(heavy_key, (N_SEGMENT, 1, 1), 0, N_DP).astype(jnp.int32)
    owner_iota = jnp.arange(N_DP, dtype=jnp.int32)[None, None, :]
    scores = jax.random.randint(order_key, (N_SEGMENT, N_DP, N_DP), 0, 1 << 20) * N_DP + owner_iota
    selected = jnp.argsort(scores, axis=-1).astype(jnp.int32)[:, :, :REQ_PRE]
    has_heavy = jnp.any(selected == heavy, axis=-1, keepdims=True)
    slot = jax.random.randint(slot_key, (N_SEGMENT, N_DP, 1), 0, REQ_PRE)
    request_iota = jnp.arange(REQ_PRE, dtype=jnp.int32)[None, None, :]
    replace = jnp.logical_not(has_heavy) & (request_iota == slot)
    return jnp.where(replace, heavy, selected).astype(jnp.int32)


def levels(own_key, shape, cuts, least, high):
    def one(dim, parts):
        steps = jax.random.uniform(jax.random.fold_in(jax.random.fold_in(own_key, 6), dim), (parts,), jnp.float32, least / len(cuts), high / len(cuts))
        return jnp.repeat(jnp.exp(steps), shape[dim] // parts).reshape((-1,) + (1,) * (len(shape) - dim - 1))

    loudness = one(*cuts[0])
    for cut in cuts[1:]:
        loudness = loudness * one(*cut)
    return loudness


def distinct(key, rows, count, top, lift):
    order = jax.random.permutation(jax.random.fold_in(key, 1), count)
    boost = order
    for power in range(3):
        boost = boost * boost // count
    boost = boost * lift // count
    chance = jax.random.randint(jax.random.fold_in(key, 2), (rows, count), 0, 4096) + boost
    holders = jax.random.permutation(jax.random.fold_in(key, 3), rows)[jnp.arange(count) % rows]
    chance = jnp.where(jnp.arange(rows)[:, None] == holders[None, :], 1 << 14, chance)
    merit = chance * count + jnp.arange(count)
    return lax.top_k(merit.astype(jnp.int32), top)[1].astype(jnp.int32)


def normal_values(rng, extent, deviation, bound, cuts=(), kind=jnp.bfloat16):
    loudness = levels(rng, extent, cuts, -0.22, 0.18) if cuts else 1.0
    result = jax.random.normal(rng, extent, jnp.float32) * deviation * loudness
    return jnp.minimum(jnp.maximum(result, -bound), bound).astype(kind)


def setup_inputs(seed: int = 0) -> dict:
    arg_keys = jax.random.split(jax.random.key(seed), 13)
    return {
        "cache_values": draw_cache_values(jax.random.fold_in(arg_keys[12], 71), 0),
        "cache_rope": normal_values(arg_keys[1], (N_SEGMENT, N_DP, REQ_PRE, ROPE, CTX), 1.0, 6.0, ((0, 2), (1, 4), (4, 64))),
        "cache_scales": jnp.clip(jnp.exp(math.log(3.0) - 2.306499 * jax.random.uniform(arg_keys[2], (N_SEGMENT, N_DP, REQ_PRE, SCALES, CTX), jnp.float32) ** levels(arg_keys[2], (N_SEGMENT, N_DP, REQ_PRE, SCALES, CTX), ((0, 2), (1, 4), (4, 64)), -0.2, 0.2)), 0.29882812, 3.0).astype(jnp.bfloat16),
        "queries": draw_queries(jax.random.fold_in(arg_keys[12], 71), 0),
        "new_keys": normal_values(arg_keys[4], (N_SEGMENT, N_DP, REQ_PRE, NEWP, QKD), 3.0, 16.0, ((0, 2), (1, 4))),
        "hidden_rows": normal_values(arg_keys[5], (N_SEGMENT, N_DP, REQ_PRE, NEWP, D), 1.0, 6.0, ((0, 2), (1, 4))),
        "expert_ids": distinct(arg_keys[6], N_SEGMENT * N_DP * REQ_PRE * NEWP, EXP_DEV * N_EP, TOPK, 512).reshape((N_SEGMENT, N_DP, REQ_PRE, NEWP, TOPK)),
        "expert_gates": jnp.clip(0.099609375 + 0.9003906 * jax.random.uniform(arg_keys[7], (N_SEGMENT, N_DP, REQ_PRE, NEWP, TOPK), jnp.float32) ** levels(arg_keys[7], (N_SEGMENT, N_DP, REQ_PRE, NEWP, TOPK), ((0, 2), (1, 4)), -0.2, 0.2), 0.099609375, 1.0).astype(jnp.bfloat16),
        "owners": draw_owners(jax.random.fold_in(arg_keys[12], 71), 0),
        "lengths": draw_lengths(jax.random.fold_in(arg_keys[12], 71), 0),
        "up_weight": normal_values(arg_keys[10], (EXP_DEV * N_EP, D, FF), D ** -0.5, 0.09375, ((0, 64), (2, 8))),
        "down_weight": normal_values(arg_keys[11], (EXP_DEV * N_EP, FF, D), FF ** -0.5, 0.1875, ((0, 64), (1, 8))),
    }


score_scale = 192.0 ** -0.5
block_width = 128
far_below = -1.0e30


def dequantize(stored, block_scales):
    positions = stored.shape[0]
    blocked = stored.astype(jnp.float32).reshape((positions, block_scales.shape[0], block_width))
    factor = jnp.transpose(block_scales.astype(jnp.float32))[:, :, None]
    return (blocked * factor).reshape((positions, stored.shape[1])).astype(jnp.bfloat16)


def block_terms(block_scores, valid_keys, key_values):
    masked = jnp.where(valid_keys, block_scores, far_below)
    peak_score = jnp.max(masked, axis=0)
    weights = jnp.where(valid_keys, jnp.exp(masked - peak_score[None, :]), 0.0)
    weight_sum = jnp.sum(weights, axis=0)
    block_out = jnp.dot(jnp.transpose(weights.astype(jnp.bfloat16)), key_values, preferred_element_type=jnp.float32)
    return peak_score, weight_sum, block_out


def join_terms(first, second):
    top_score = jnp.maximum(first[0], second[0])
    early_factor = jnp.exp(first[0] - top_score)
    late_factor = jnp.exp(second[0] - top_score)
    return (top_score, first[1] * early_factor + second[1] * late_factor,
            first[2] * early_factor[:, None] + second[2] * late_factor[:, None])


def attend(request):
    stored, rotary, block_scales, query_cols, fresh_keys, length_now = request
    latent = dequantize(stored, block_scales)
    column_pos = jnp.arange(NEWP * H, dtype=jnp.int32) // H
    fresh_pos = jnp.arange(NEWP, dtype=jnp.int32)
    fresh_scores = jnp.dot(fresh_keys, query_cols, preferred_element_type=jnp.float32) * score_scale
    fresh_valid = fresh_pos[:, None] <= column_pos[None, :]
    state = block_terms(fresh_scores, fresh_valid, fresh_keys[:, :LAT])

    def scan_step(carry, block_index):
        start = (block_index * CTX_DEV).astype(jnp.int32)
        latent_part = lax.dynamic_slice_in_dim(latent, start, CTX_DEV, 0)
        rotary_part = lax.dynamic_slice_in_dim(rotary, start, CTX_DEV, 1)
        block_scores = (jnp.dot(latent_part, query_cols[:LAT], preferred_element_type=jnp.float32)
                        + jnp.dot(jnp.transpose(rotary_part), query_cols[LAT:], preferred_element_type=jnp.float32)) * score_scale
        position = start + jnp.arange(CTX_DEV, dtype=jnp.int32)
        valid_keys = jnp.broadcast_to((position < length_now)[:, None], block_scores.shape)
        return join_terms(carry, block_terms(block_scores, valid_keys, latent_part)), None

    state, _ = lax.scan(scan_step, state, jnp.arange(N_EP, dtype=jnp.int32))
    return state[2] / state[1][:, None]


def expert_rows(token_rows, chosen, gate_values, up_weight, down_weight):
    def scan_step(running, expert):
        weight = jnp.sum(jnp.where(chosen == expert, gate_values.astype(jnp.float32), 0.0), axis=1)
        hidden = jax.nn.silu(jnp.dot(token_rows, up_weight[expert], preferred_element_type=jnp.float32)).astype(jnp.bfloat16)
        output = jnp.dot(hidden, down_weight[expert], preferred_element_type=jnp.float32)
        return running + weight[:, None] * output, None

    start_sum = jnp.zeros((token_rows.shape[0], token_rows.shape[1]), jnp.float32)
    running, _ = lax.scan(scan_step, start_sum, jnp.arange(up_weight.shape[0], dtype=jnp.int32))
    return running


def reference(cache_values, cache_rope, cache_scales, queries, new_keys, hidden_rows, expert_ids, expert_gates, owners, lengths, up_weight, down_weight):
    request_count = N_SEGMENT * N_DP * REQ_PRE
    flat = (cache_values.reshape((request_count, CTX, LAT)),
            cache_rope.reshape((request_count, ROPE, CTX)),
            cache_scales.reshape((request_count, SCALES, CTX)),
            queries.reshape((request_count, QKD, NEWP * H)),
            new_keys.reshape((request_count, NEWP, QKD)),
            lengths.reshape((request_count,)))
    attended = lax.map(attend, flat).reshape((N_SEGMENT, N_DP, REQ_PRE, NEWP, H, LAT)).astype(jnp.bfloat16)
    mixed = expert_rows(hidden_rows.reshape((request_count * NEWP, D)),
                        expert_ids.reshape((request_count * NEWP, TOPK)),
                        expert_gates.reshape((request_count * NEWP, TOPK)),
                        up_weight, down_weight)
    mixed = mixed.reshape((N_SEGMENT, N_DP, REQ_PRE, NEWP, D)).astype(jnp.bfloat16)
    section = jnp.broadcast_to((N_SEGMENT - 1 - jnp.arange(N_SEGMENT, dtype=jnp.int32))[:, None, None], owners.shape)
    source = jnp.broadcast_to(jnp.arange(N_DP, dtype=jnp.int32)[None, :, None], owners.shape)
    attention = jnp.zeros((N_SEGMENT, N_DP, N_DP, NEWP, H, LAT), jnp.bfloat16).at[section, owners, source].set(attended)
    expert_mix = jnp.zeros((N_SEGMENT, N_DP, N_DP, NEWP, D), jnp.bfloat16).at[section, owners, source].set(mixed)
    return attention, expert_mix
```

```python
import functools

import jax
import jax.numpy as jnp
from jax import lax
from jax.experimental import pallas as pl
from jax.experimental.pallas import tpu as pltpu
from jax.sharding import PartitionSpec as P

score_scale = 192.0 ** (-0.5)
far_below = -1e30
x_chips = 4
MESH = pl.DeviceIdType.MESH
f32 = jnp.float32
bf16 = jnp.bfloat16


def iota(shape, dim):
    return lax.broadcasted_iota(jnp.int32, shape, dim)


def dot(a, b):
    return jnp.dot(a, b, preferred_element_type=f32)


def dot_rows(a, b):
    return lax.dot_general(a, b, (((1,), (1,)), ((), ())), preferred_element_type=f32)


def dot_cols(a, b):
    return lax.dot_general(a, b, (((0,), (0,)), ((), ())), preferred_element_type=f32)


def three_parts(value):
    high = value.astype(bf16).astype(f32)
    rest = value - high
    middle = rest.astype(bf16).astype(f32)
    low = (rest - middle).astype(bf16).astype(f32)
    return high, middle, low


def kernel(
    sizes,
    cv_h, q_h, up_h, dn_h, cr, cs, nk, xr, ids, gates, owners, lengths,
    attn_o, mix_o,
    cv, q, up, dn, tr, nkp, xf, xg,
    a1s, a1r, t1s, t1r, a2s, a2r, a3s, a3r,
    e1s, e1r, e2s, e2r, e3s, e3r, e4, e4f, e5x, e5y,
    in_sem,
    e0_ss, e0_rs, a1_ss, a1_rs, t1_ss, t1_rs, a2_ss, a2_rs, a3_ss, a3_rs,
    e1_ss, e1_rs, e2_ss, e2_rs, e3_ss, e3_rs, e4_ss, e4_rs, e5x_ss, e5x_rs, e5y_ss, e5y_rs,
):
    nd, ny, nz, nx = sizes
    s, y, ep = lax.axis_index("segment"), lax.axis_index("dp"), lax.axis_index("ep")
    z, x = ep // nx, lax.rem(ep, nx)
    d = s * ny + y
    ctx, lat = cv.shape[1], cv.shape[2]
    cols = q.shape[2]
    heads = cols // 2
    hl = heads // (nz * nx)
    width = up.shape[1]
    quarter = width // 4
    ycols = width // ny
    xcols = e2s.shape[2]
    rows_x = a1s.shape[1]
    sec = ny * 4

    loads = [
        pltpu.make_async_copy(a, b, in_sem.at[i])
        for i, (a, b) in enumerate(((cv_h, cv), (q_h, q), (up_h, up), (dn_h, dn)))
    ]
    for load in loads:
        load.start()

    def plane(k):
        to = lax.rem(d + k, nd)
        return to, {"segment": to // ny, "dp": lax.rem(to, ny)}

    def along_x(k):
        to = lax.rem(x + k, nx)
        return to, {"ep": z * nx + to}

    def along_z(k):
        to = lax.rem(z + k, nz)
        return to, {"ep": to * nx + x}

    def along_y(k):
        to = lax.rem(y + k, ny)
        return to, {"dp": to}

    def across(k):
        to = lax.rem(y + k, ny)
        return to, {"segment": 1 - s, "dp": to}

    def remote(src, dst, ss, rs, k, to):
        return pltpu.make_async_remote_copy(
            src_ref=src, dst_ref=dst, send_sem=ss.at[k], recv_sem=rs.at[k],
            device_id=to, device_id_type=MESH,
        )

    def c_e0(k):
        return remote(xg.at[d], xg.at[d], e0_ss, e0_rs, k, plane(k)[1])

    def c_a1(k):
        to, dev = along_x(k)
        return remote(a1s.at[to], a1r.at[k], a1_ss, a1_rs, k, dev)

    def c_t1(k):
        to, dev = along_x(k)
        return remote(t1s.at[to], t1r.at[k], t1_ss, t1_rs, k, dev)

    def c_a2(k):
        to, dev = along_z(k)
        return remote(a2s.at[to], a2r.at[k], a2_ss, a2_rs, k, dev)

    def c_a3(k):
        return remote(a3s, a3r.at[y], a3_ss, a3_rs, k, across(k)[1])

    def c_e1(k):
        to, dev = plane(k)
        return remote(e1s.at[to], e1r.at[k], e1_ss, e1_rs, k, dev)

    def c_e2(k):
        to, dev = along_x(k)
        return remote(e2s.at[to], e2r.at[k], e2_ss, e2_rs, k, dev)

    def c_e3(k):
        to, dev = along_z(k)
        return remote(e3s.at[to], e3r.at[k], e3_ss, e3_rs, k, dev)

    def c_e4(k):
        return remote(e4.at[z], e4.at[z], e4_ss, e4_rs, k, along_z(k)[1])

    def c_e5x(k):
        return remote(e5x.at[x], e5x.at[x], e5x_ss, e5x_rs, k, along_x(k)[1])

    def c_e5y(k):
        return remote(e5y.at[y], e5y.at[y], e5y_ss, e5y_rs, k, along_y(k)[1])

    def each(first, last, act):
        def body(k, carry):
            act(k)
            return carry

        lax.fori_loop(first, last, body, 0)

    barrier = pltpu.get_barrier_semaphore()

    def greet(where):
        def act(k):
            pl.semaphore_signal(barrier, inc=1, device_id=where(k)[1], device_id_type=MESH)

        return act

    each(1, nd, greet(plane))
    each(1, nx, greet(along_x))
    each(1, nz, greet(along_z))

    xf[...] = jnp.zeros_like(xf)
    for r in range(2):
        for j in range(2):
            i = 2 * r + j
            row = xr[r, j:j + 1, :].astype(f32)
            for part in range(4):
                xf[4 * i + part:4 * i + part + 1, :quarter] = row[:, part * quarter:(part + 1) * quarter]
            xf[4 * i:4 * i + 1, quarter:quarter + 8] = ids[r, j:j + 1, :].astype(f32)
            xf[4 * i + 1:4 * i + 2, quarter:quarter + 8] = gates[r, j:j + 1, :].astype(f32)
            xf[4 * i + 2:4 * i + 3, quarter:] = jnp.full((1, 128), owners[r], jnp.int32).astype(f32)
    xg[d] = xf[...].astype(bf16)

    pl.semaphore_wait(barrier, (nd - 1) + (nx - 1) + (nz - 1))
    each(1, nd, lambda k: c_e0(k).start())

    tr[...] = jnp.zeros_like(tr)
    nkp[...] = jnp.zeros_like(nkp)
    for r in range(2):
        tr[8 * r:8 * r + 4, :ctx] = cs[r].astype(f32)
        nkp[16 * r:16 * r + 2, :] = nk[r].astype(f32)
    scale_cols = tr[:, :ctx].T
    total_rows = nx * rows_x
    place = iota((total_rows, cols), 0)
    per = 2 * hl
    h_of = lax.rem(place, hl)
    j_of = lax.rem(place // hl, 2)
    r_of = lax.rem(place // per, 2)
    z_of = lax.rem(place // (2 * per), nz)
    x_of = place // (2 * per * nz)
    match = (j_of * heads + (z_of * nx + x_of) * hl + h_of) == iota((total_rows, cols), 1)
    loads[0].wait()
    loads[1].wait()
    out = jnp.zeros((total_rows, lat), f32)
    stats = jnp.zeros((16, total_rows), f32)
    for r in range(2):
        latent = jnp.concatenate(
            [
                cv[r, :, b * 128:(b + 1) * 128].astype(f32) * scale_cols[:, 8 * r + b:8 * r + b + 1]
                for b in range(lat // 128)
            ],
            axis=1,
        ).astype(bf16)
        fresh = nkp[16 * r:16 * r + 16, :].astype(bf16)
        cached = dot(latent, q[r, :lat, :]) + dot_cols(cr[r], q[r, lat:, :])
        newer = dot(fresh[:, :lat], q[r, :lat, :]) + dot(fresh[:, lat:], q[r, lat:, :])
        cached_ok = ep * ctx + iota((ctx, cols), 0) < lengths[r]
        newer_ok = (iota((16, cols), 0) + jnp.where(ep == 0, 0, 16)) <= (iota((16, cols), 1) // heads)
        cached = jnp.where(cached_ok, cached * score_scale, far_below)
        newer = jnp.where(newer_ok, newer * score_scale, far_below)
        peak = jnp.maximum(
            jnp.max(cached, axis=0, keepdims=True), jnp.max(newer, axis=0, keepdims=True)
        )
        cached = jnp.where(cached_ok, jnp.exp(cached - peak), 0.0)
        newer = jnp.where(newer_ok, jnp.exp(newer - peak), 0.0)
        total = jnp.sum(cached, axis=0, keepdims=True) + jnp.sum(newer, axis=0, keepdims=True)
        line = iota((16, cols), 0)
        extra = jnp.zeros((16, cols), f32)
        for n, part in enumerate(three_parts(peak) + three_parts(total)):
            extra = jnp.where(line == n, part, extra)
        order = jnp.where(match & (r_of == r), 1.0, 0.0).astype(bf16)
        out = out + dot(dot_rows(order, cached.astype(bf16)).astype(bf16), latent)
        out = out + dot(dot_rows(order, newer.astype(bf16)).astype(bf16), fresh[:, :lat])
        stats = stats + dot_rows(extra.astype(bf16), order)
    peak = stats[0:1] + stats[1:2] + stats[2:3]
    total = stats[3:4] + stats[4:5] + stats[5:6]
    for to in range(nx):
        a1s[to] = out[to * rows_x:(to + 1) * rows_x].astype(bf16)
        t1s[to, 0:1, :] = peak[:, to * rows_x:(to + 1) * rows_x]
        t1s[to, 1:2, :] = total[:, to * rows_x:(to + 1) * rows_x]
        t1s[to, 2:8, :] = jnp.zeros((6, rows_x), f32)
    each(1, nx, lambda k: c_t1(k).start())
    each(1, nx, lambda k: c_a1(k).start())

    each(1, nd, lambda k: c_e0(k).wait_recv())
    loads[2].wait()
    loads[3].wait()
    gathered = xg[...].reshape((nd * 16, xg.shape[2]))
    notes = gathered[:, quarter:]
    row_count = nd * 4
    want = iota((3 * row_count, nd * 16), 0)
    pick = iota((3 * row_count, nd * 16), 1) == 4 * lax.rem(want, row_count) + want // row_count
    pick = jnp.where(pick, 1.0, 0.0).astype(bf16)
    routing = dot(pick, notes)
    chosen, gate_values = routing[:row_count], routing[row_count:2 * row_count]
    lane = iota((row_count, 128), 1)
    part_of = lax.rem(iota((nd * 16, up.shape[2]), 0), 4)
    partial = jnp.zeros((row_count, width), f32)
    for e in range(up.shape[0]):
        expert = (ep * up.shape[0] + e).astype(f32)
        gate = jnp.sum(
            jnp.where((chosen == expert) & (lane < 8), gate_values, 0.0), axis=1, keepdims=True
        )
        acc = jnp.zeros((nd * 16, up.shape[2]), f32)
        for part in range(4):
            piece = dot(gathered[:, :quarter], up[e, part * quarter:(part + 1) * quarter, :])
            acc = jnp.where(part_of == part, piece, acc)
        acc = acc + pltpu.roll(acc, nd * 16 - 1, 0)
        acc = acc + pltpu.roll(acc, nd * 16 - 2, 0)
        hidden = (acc / (1.0 + jnp.exp(-acc))).astype(bf16)
        hidden = dot(pick[:row_count], hidden).astype(bf16)
        partial = partial + gate * dot(hidden, dn[e])
    for c in range(2):
        for to in range(ny):
            e1s[c * ny + to] = partial[
                (1 - c) * sec:(2 - c) * sec, to * ycols:(to + 1) * ycols
            ].astype(bf16)
    each(1, nd, lambda k: c_e1(k).start())

    first_row = jnp.where(s == 0, ny * 16, 0)
    owner_lane = jnp.where(iota((16, 128), 1) == 0, 1.0, 0.0).astype(bf16)

    def owner_row(count, split):
        row = iota((count, nd * 16), 0)
        spot = first_row + 4 * (row // split) + 2
        pull = jnp.where(iota((count, nd * 16), 1) == spot, 1.0, 0.0).astype(bf16)
        return dot_rows(owner_lane, dot(pull, notes).astype(bf16))[0:1]

    mine = y.astype(f32)
    out_i, in_i = iota((2 * ny, sec), 0), iota((2 * ny, sec), 1)
    mix_pick = (out_i // 2 == in_i // 4) & (lax.rem(out_i, 2) == lax.rem(in_i, 2))
    mix_pick = jnp.where(mix_pick & (owner_row(sec, 1) == mine), 1.0, 0.0).astype(bf16)
    out_i, in_i = iota((2 * per // 2 * ny, 2 * per * ny), 0), iota((2 * per // 2 * ny, 2 * per * ny), 1)
    attn_pick = (out_i // per == in_i // (2 * per)) & (lax.rem(out_i, per) == lax.rem(in_i, per))
    attn_pick = jnp.where(attn_pick & (owner_row(2 * per * ny, hl) == mine), 1.0, 0.0).astype(bf16)

    each(1, nx, lambda k: c_t1(k).wait_recv())
    tops = [t1s[x, 0:1, :]] + [t1r[k, 0:1, :] for k in range(1, nx)]
    sums = [t1s[x, 1:2, :]] + [t1r[k, 1:2, :] for k in range(1, nx)]
    top = functools.reduce(jnp.maximum, tops)
    factors = [jnp.exp(one - top) for one in tops]
    total = functools.reduce(jnp.add, [a * b for a, b in zip(factors, sums)])
    tr[...] = jnp.zeros_like(tr)
    for n, one in enumerate(list(three_parts(top) + three_parts(total)) + factors):
        tr[n:n + 1, :rows_x] = one
    turned = tr[:, :rows_x].T
    each(1, nx, lambda k: c_a1(k).wait_recv())
    merged = turned[:, 6:7] * a1s[x].astype(f32)
    for k in range(1, nx):
        merged = merged + turned[:, 6 + k:7 + k] * a1r[k].astype(f32)
    a2s[:, :, :lat] = merged.reshape((nz, 2 * per, lat)).astype(bf16)
    a2s[:, :, lat:] = turned.reshape((nz, 2 * per, 128)).astype(bf16)
    each(1, nz, lambda k: c_a2(k).start())

    each(1, nd, lambda k: c_e1(k).wait_recv())
    summed = e1s[d].astype(f32)
    for k in range(1, nd):
        summed = summed + e1r[k].astype(f32)
    for to in range(nx):
        low, high = to * xcols, min((to + 1) * xcols, ycols)
        e2s[to, :, :high - low] = summed[:, low:high].astype(bf16)
        if high - low < xcols:
            e2s[to, :, high - low:] = jnp.zeros((sec, xcols - (high - low)), bf16)
    each(1, nx, lambda k: c_e2(k).start())
    each(1, nx, lambda k: c_e2(k).wait_recv())
    summed = e2s[x].astype(f32)
    for k in range(1, nx):
        summed = summed + e2r[k].astype(f32)
    rz = sec // nz
    for to in range(nz):
        e3s[to] = summed[to * rz:(to + 1) * rz]
    each(1, nz, lambda k: c_e3(k).start())
    each(1, nz, lambda k: c_e3(k).wait_recv())
    summed = e3s[z]
    for k in range(1, nz):
        summed = summed + e3r[k]
    e4[z] = summed
    each(1, nz, lambda k: c_e4(k).start())

    a2r[0] = a2s[z]
    each(1, nz, lambda k: c_a2(k).wait_recv())
    arrived = a2r[...].astype(f32)
    tops = arrived[:, :, lat:lat + 1] + arrived[:, :, lat + 1:lat + 2] + arrived[:, :, lat + 2:lat + 3]
    sums = arrived[:, :, lat + 3:lat + 4] + arrived[:, :, lat + 4:lat + 5] + arrived[:, :, lat + 5:lat + 6]
    factors = jnp.exp(tops - jnp.max(tops, axis=0, keepdims=True))
    total = jnp.sum(factors * sums, axis=0)
    a3s[...] = (jnp.sum(factors * arrived[:, :, :lat], axis=0) / total).astype(bf16)
    each(0, ny, lambda k: c_a3(k).start())

    each(1, nz, lambda k: c_e4(k).wait_recv())
    for k in range(nz):
        e4f[k * rz:(k + 1) * rz, :] = e4[k]
    e5x[x] = e4f[...].astype(bf16)
    each(1, nx, lambda k: c_e5x(k).start())
    each(1, nx, lambda k: c_e5x(k).wait_recv())
    for k in range(nx):
        low, high = k * xcols, min((k + 1) * xcols, ycols)
        e5y[y, :, low:high] = e5x[k, :, :high - low]
    each(1, ny, lambda k: c_e5y(k).start())

    each(0, ny, lambda k: c_a3(k).wait_recv())
    finished = a3r[...].astype(f32).reshape((ny * 2 * per, lat)).astype(bf16)
    attn_o[...] = dot(attn_pick, finished).astype(bf16)

    each(1, ny, lambda k: c_e5y(k).wait_recv())
    for k in range(ny):
        mix_o[:, k * ycols:(k + 1) * ycols] = dot(mix_pick, e5y[k]).astype(bf16)

    def finish(k, carry):
        return carry

    each(1, nd, lambda k: c_e0(k).wait_send())
    each(1, nx, lambda k: c_t1(k).wait_send())
    each(1, nx, lambda k: c_a1(k).wait_send())
    each(1, nz, lambda k: c_a2(k).wait_send())
    each(0, ny, lambda k: c_a3(k).wait_send())
    each(1, nd, lambda k: c_e1(k).wait_send())
    each(1, nx, lambda k: c_e2(k).wait_send())
    each(1, nz, lambda k: c_e3(k).wait_send())
    each(1, nz, lambda k: c_e4(k).wait_send())
    each(1, nx, lambda k: c_e5x(k).wait_send())
    each(1, ny, lambda k: c_e5y(k).wait_send())


def shards(
    cache_values, cache_rope, cache_scales, queries, new_keys, hidden_rows,
    expert_ids, expert_gates, owners, lengths, up_weight, down_weight,
):
    ny = lax.axis_size("dp")
    nd = ny * lax.axis_size("segment")
    nx = x_chips
    nz = lax.axis_size("ep") // nx
    cv, cr, cs, q = cache_values[0, 0], cache_rope[0, 0], cache_scales[0, 0], queries[0, 0]
    nk, xr, ids, gates = new_keys[0, 0], hidden_rows[0, 0], expert_ids[0, 0], expert_gates[0, 0]
    ctx, lat = cv.shape[1:]
    cols = q.shape[2]
    heads = cols // 2
    hl = heads // (nz * nx)
    width = up_weight.shape[1]
    ycols = width // ny
    xcols = -(-ycols // (nx * 128)) * 128
    sec = ny * 4
    rows_x = nz * 4 * hl
    vmem = pl.BlockSpec(memory_space=pltpu.VMEM)
    smem = pl.BlockSpec(memory_space=pltpu.SMEM)
    anywhere = pl.BlockSpec(memory_space=pl.ANY)
    sems = lambda n: pltpu.SemaphoreType.DMA((n,))
    attention, mix = pl.pallas_call(
        functools.partial(kernel, (nd, ny, nz, nx)),
        out_shape=(
            jax.ShapeDtypeStruct((ny * 2 * hl, lat), bf16),
            jax.ShapeDtypeStruct((ny * 2, width), bf16),
        ),
        in_specs=[anywhere] * 4 + [vmem] * 6 + [smem] * 2,
        out_specs=(vmem, vmem),
        scratch_shapes=[
            pltpu.VMEM(cv.shape, bf16),
            pltpu.VMEM(q.shape, bf16),
            pltpu.VMEM(up_weight.shape, bf16),
            pltpu.VMEM(down_weight.shape, bf16),
            pltpu.VMEM((128, 128), f32),
            pltpu.VMEM((32, nk.shape[2]), f32),
            pltpu.VMEM((16, width // 4 + 128), f32),
            pltpu.VMEM((nd, 16, width // 4 + 128), bf16),
            pltpu.VMEM((nx, rows_x, lat), bf16),
            pltpu.VMEM((nx, rows_x, lat), bf16),
            pltpu.VMEM((nx, 8, rows_x), f32),
            pltpu.VMEM((nx, 8, rows_x), f32),
            pltpu.VMEM((nz, 4 * hl, lat + 128), bf16),
            pltpu.VMEM((nz, 4 * hl, lat + 128), bf16),
            pltpu.VMEM((4 * hl, lat), bf16),
            pltpu.VMEM((ny, 4 * hl, lat), bf16),
            pltpu.VMEM((nd, sec, ycols), bf16),
            pltpu.VMEM((nd, sec, ycols), bf16),
            pltpu.VMEM((nx, sec, xcols), bf16),
            pltpu.VMEM((nx, sec, xcols), bf16),
            pltpu.VMEM((nz, sec // nz, xcols), f32),
            pltpu.VMEM((nz, sec // nz, xcols), f32),
            pltpu.VMEM((nz, sec // nz, xcols), f32),
            pltpu.VMEM((sec, xcols), f32),
            pltpu.VMEM((nx, sec, xcols), bf16),
            pltpu.VMEM((ny, sec, ycols), bf16),
            sems(4),
            sems(nd), sems(nd), sems(nx), sems(nx), sems(nx), sems(nx), sems(nz), sems(nz),
            sems(ny), sems(ny),
            sems(nd), sems(nd), sems(nx), sems(nx), sems(nz), sems(nz), sems(nz), sems(nz),
            sems(nx), sems(nx), sems(ny), sems(ny),
        ],
        compiler_params=pltpu.CompilerParams(
            collective_id=0, has_side_effects=True, vmem_limit_bytes=60 * 1024 * 1024
        ),
    )(cv, q, up_weight, down_weight, cr, cs, nk, xr, ids, gates, owners[0, 0], lengths[0, 0])
    return (
        attention.reshape((1, 1, ny, 2, hl, lat)),
        mix.reshape((1, 1, ny, 2, width)),
    )


def solution(mesh):
    placed = (
        P("segment", "dp", None, "ep", None),
        P("segment", "dp", None, None, "ep"),
        P("segment", "dp", None, None, "ep"),
        P("segment", "dp", None, None, None),
        P("segment", "dp", None, None, None),
        P("segment", "dp", None, None, None),
        P("segment", "dp", None, None, None),
        P("segment", "dp", None, None, None),
        P("segment", "dp", None),
        P("segment", "dp", None),
        P("ep", None, ("segment", "dp")),
        P("ep", ("segment", "dp"), None),
    )
    return jax.shard_map(
        shards,
        mesh=mesh,
        in_specs=placed,
        out_specs=(
            P("segment", "dp", None, None, "ep", None),
            P("segment", "dp", None, None, None),
        ),
        check_vma=False,
    )
```

```python
import functools

import jax
import jax.numpy as jnp
from jax import lax
from jax.experimental import pallas as pl
from jax.experimental.pallas import tpu as pltpu
from jax.sharding import PartitionSpec as P

score_scale = 192.0 ** (-0.5)
far_below = -1e30
x_chips = 4
MESH = pl.DeviceIdType.MESH
f32 = jnp.float32
bf16 = jnp.bfloat16


def iota(shape, dim):
    return lax.broadcasted_iota(jnp.int32, shape, dim)


def dot(a, b):
    return jnp.dot(a, b, preferred_element_type=f32)


def dot_rows(a, b):
    return lax.dot_general(a, b, (((1,), (1,)), ((), ())), preferred_element_type=f32)


def dot_cols(a, b):
    return lax.dot_general(a, b, (((0,), (0,)), ((), ())), preferred_element_type=f32)


def three_parts(value):
    high = value.astype(bf16).astype(f32)
    rest = value - high
    middle = rest.astype(bf16).astype(f32)
    low = (rest - middle).astype(bf16).astype(f32)
    return high, middle, low


def kernel(
    sizes,
    cv_h, q_h, up_h, dn_h, cr, cs, nk, xr, ids, gates, owners, lengths,
    attn_o, mix_o,
    cv, q, up, dn, tr, nkp, xf, xg,
    a1s, a1r, t1s, t1r, a2s, a2r, a3s, a3r,
    e1s, e1r, e2s, e2r, e3s, e3r, e5,
    in_sem,
    e0_ss, e0_rs, a1_ss, a1_rs, t1_ss, t1_rs, a2_ss, a2_rs, a3_ss, a3_rs,
    e1_ss, e1_rs, e2_ss, e2_rs, e3_ss, e3_rs, e5_ss, e5_rs,
):
    nd, ny, nz, nx = sizes
    s, y, ep = lax.axis_index("segment"), lax.axis_index("dp"), lax.axis_index("ep")
    z, x = ep // nx, lax.rem(ep, nx)
    d = s * ny + y
    ctx, lat = cv.shape[1], cv.shape[2]
    cols = q.shape[2]
    heads = cols // 2
    hl = heads // (nz * nx)
    width = up.shape[1]
    quarter = width // 4
    nxy = nx * ny
    spot = y * nx + x
    block = e2s.shape[2]
    rows_x = a1s.shape[1]
    sec = ny * 4

    loads = [
        pltpu.make_async_copy(a, b, in_sem.at[i])
        for i, (a, b) in enumerate(((cv_h, cv), (q_h, q), (up_h, up), (dn_h, dn)))
    ]
    for load in loads:
        load.start()

    def plane(k):
        to = lax.rem(d + k, nd)
        return to, {"segment": to // ny, "dp": lax.rem(to, ny)}

    def along_x(k):
        to = lax.rem(x + k, nx)
        return to, {"ep": z * nx + to}

    def along_z(k):
        to = lax.rem(z + k, nz)
        return to, {"ep": to * nx + x}

    def along_xy(k):
        to_y = lax.rem(y + k // nx, ny)
        to_x = lax.rem(x + k % nx, nx)
        return to_y * nx + to_x, {"dp": to_y, "ep": z * nx + to_x}

    def across(k):
        to = lax.rem(y + k, ny)
        return to, {"segment": 1 - s, "dp": to}

    def remote(src, dst, ss, rs, k, to):
        return pltpu.make_async_remote_copy(
            src_ref=src, dst_ref=dst, send_sem=ss.at[k], recv_sem=rs.at[k],
            device_id=to, device_id_type=MESH,
        )

    def c_e0(k):
        return remote(xg.at[d], xg.at[d], e0_ss, e0_rs, k, plane(k)[1])

    def c_a1(k):
        to, dev = along_x(k)
        return remote(a1s.at[to], a1r.at[k], a1_ss, a1_rs, k, dev)

    def c_t1(k):
        to, dev = along_x(k)
        return remote(t1s.at[to], t1r.at[k], t1_ss, t1_rs, k, dev)

    def c_a2(k):
        to, dev = along_z(k)
        return remote(a2s.at[to], a2r.at[k], a2_ss, a2_rs, k, dev)

    def c_a3(k):
        return remote(a3s, a3r.at[y], a3_ss, a3_rs, k, across(k)[1])

    def c_e1(k):
        return remote(e1s, e1r, e1_ss, e1_rs, k, {"segment": 1 - s})

    def c_e2(k):
        to, dev = along_xy(k)
        return remote(e2s.at[to], e2r.at[k], e2_ss, e2_rs, k, dev)

    def c_e3(k):
        return remote(e3s, e3r.at[k], e3_ss, e3_rs, k, along_z(k)[1])

    def c_e5(k):
        return remote(e5.at[spot], e5.at[spot], e5_ss, e5_rs, k, along_xy(k)[1])

    def each(first, last, act):
        for k in range(first, last):
            act(k)

    barrier = pltpu.get_barrier_semaphore()

    def greet(where):
        def act(k):
            pl.semaphore_signal(barrier, inc=1, device_id=where(k)[1], device_id_type=MESH)

        return act

    each(1, nz, greet(along_z))
    each(1, nd, greet(plane))
    for k in range(1, nxy):
        if k % nx:
            greet(along_xy)(k)

    xf[...] = jnp.zeros_like(xf)
    for r in range(2):
        for j in range(2):
            i = 2 * r + j
            row = xr[r, j:j + 1, :].astype(f32)
            for part in range(4):
                xf[4 * i + part:4 * i + part + 1, :quarter] = row[:, part * quarter:(part + 1) * quarter]
            xf[4 * i:4 * i + 1, quarter:quarter + 8] = ids[r, j:j + 1, :].astype(f32)
            xf[4 * i + 1:4 * i + 2, quarter:quarter + 8] = gates[r, j:j + 1, :].astype(f32)
            xf[4 * i + 2:4 * i + 3, quarter:] = jnp.full((1, 128), owners[r], jnp.int32).astype(f32)
    xg[d] = xf[...].astype(bf16)

    tr[...] = jnp.zeros_like(tr)
    nkp[...] = jnp.zeros_like(nkp)
    for r in range(2):
        tr[8 * r:8 * r + 4, :ctx] = cs[r].astype(f32)
        nkp[16 * r:16 * r + 2, :] = nk[r].astype(f32)
    scale_cols = tr[:, :ctx].T
    total_rows = nx * rows_x
    place = iota((total_rows, cols), 0)
    per = 2 * hl
    h_of = lax.rem(place, hl)
    j_of = lax.rem(place // hl, 2)
    r_of = lax.rem(place // per, 2)
    z_of = lax.rem(place // (2 * per), nz)
    x_of = place // (2 * per * nz)
    match = (j_of * heads + (z_of * nx + x_of) * hl + h_of) == iota((total_rows, cols), 1)
    loads[0].wait()
    loads[1].wait()
    out = jnp.zeros((total_rows, lat), f32)
    stats = jnp.zeros((16, total_rows), f32)
    for r in range(2):
        latent = jnp.concatenate(
            [
                cv[r, :, b * 128:(b + 1) * 128].astype(f32) * scale_cols[:, 8 * r + b:8 * r + b + 1]
                for b in range(lat // 128)
            ],
            axis=1,
        ).astype(bf16)
        fresh = nkp[16 * r:16 * r + 16, :].astype(bf16)
        cached = dot(latent, q[r, :lat, :]) + dot_cols(cr[r], q[r, lat:, :])
        newer = dot(fresh[:, :lat], q[r, :lat, :]) + dot(fresh[:, lat:], q[r, lat:, :])
        cached_ok = ep * ctx + iota((ctx, cols), 0) < lengths[r]
        newer_ok = (iota((16, cols), 0) + jnp.where(ep == 0, 0, 16)) <= (iota((16, cols), 1) // heads)
        cached = jnp.where(cached_ok, cached * score_scale, far_below)
        newer = jnp.where(newer_ok, newer * score_scale, far_below)
        peak = jnp.maximum(
            jnp.max(cached, axis=0, keepdims=True), jnp.max(newer, axis=0, keepdims=True)
        )
        cached = jnp.where(cached_ok, jnp.exp(cached - peak), 0.0)
        newer = jnp.where(newer_ok, jnp.exp(newer - peak), 0.0)
        total = jnp.sum(cached, axis=0, keepdims=True) + jnp.sum(newer, axis=0, keepdims=True)
        line = iota((16, cols), 0)
        extra = jnp.zeros((16, cols), f32)
        for n, part in enumerate(three_parts(peak) + three_parts(total)):
            extra = jnp.where(line == n, part, extra)
        order = jnp.where(match & (r_of == r), 1.0, 0.0).astype(bf16)
        out = out + dot(dot_rows(order, cached.astype(bf16)).astype(bf16), latent)
        out = out + dot(dot_rows(order, newer.astype(bf16)).astype(bf16), fresh[:, :lat])
        stats = stats + dot_rows(extra.astype(bf16), order)
    peak = stats[0:1] + stats[1:2] + stats[2:3]
    total = stats[3:4] + stats[4:5] + stats[5:6]
    for to in range(nx):
        a1s[to] = out[to * rows_x:(to + 1) * rows_x].astype(bf16)
        t1s[to, 0:1, :] = peak[:, to * rows_x:(to + 1) * rows_x]
        t1s[to, 1:2, :] = total[:, to * rows_x:(to + 1) * rows_x]
        t1s[to, 2:8, :] = jnp.zeros((6, rows_x), f32)
    pl.semaphore_wait(barrier, (nz - 1) + (nd - 1) + (nxy - ny))
    each(1, nd, lambda k: c_e0(k).start())
    each(1, nx, lambda k: c_t1(k).start())
    each(1, nx, lambda k: c_a1(k).start())

    row_count = nd * 4
    want = iota((3 * row_count, nd * 16), 0)
    pick = iota((3 * row_count, nd * 16), 1) == 4 * lax.rem(want, row_count) + want // row_count
    pick = jnp.where(pick, 1.0, 0.0).astype(bf16)
    lane = iota((row_count, 128), 1)
    experts, hidden_width = up.shape[0], up.shape[2]
    part_of = lax.rem(iota((nd * 16, experts * hidden_width), 0), 4)
    loads[2].wait()
    loads[3].wait()
    each(1, nd, lambda k: c_e0(k).wait_recv())
    gathered = xg[...].reshape((nd * 16, xg.shape[2]))
    acc = jnp.zeros((nd * 16, experts * hidden_width), f32)
    for part in range(4):
        weights = jnp.concatenate(
            [up[e, part * quarter:(part + 1) * quarter, :] for e in range(experts)], axis=1
        )
        acc = jnp.where(part_of == part, dot(gathered[:, :quarter], weights), acc)
    notes = gathered[:, quarter:]
    routing = dot(pick, notes)
    chosen, gate_values = routing[:row_count], routing[row_count:2 * row_count]
    acc = acc + pltpu.roll(acc, nd * 16 - 1, 0)
    acc = acc + pltpu.roll(acc, nd * 16 - 2, 0)
    hidden = (acc / (1.0 + jnp.exp(-acc))).astype(bf16)
    hidden = dot(pick[:row_count], hidden).astype(bf16)
    partial = jnp.zeros((row_count, width), f32)
    for e in range(experts):
        expert = (ep * experts + e).astype(f32)
        gate = jnp.sum(
            jnp.where((chosen == expert) & (lane < 8), gate_values, 0.0), axis=1, keepdims=True
        )
        partial = partial + gate * dot(hidden[:, e * hidden_width:(e + 1) * hidden_width], dn[e])
    first, second = partial[:sec], partial[sec:]
    e1s[...] = jnp.where(s == 0, first, second).astype(bf16)
    each(1, 2, lambda k: c_e1(k).start())
    own = jnp.where(s == 0, second, first)

    each(1, 2, lambda k: c_e1(k).wait_recv())
    own = own + e1r[...].astype(f32)
    for to in range(nxy):
        low, high = to * block, min((to + 1) * block, width)
        if low < width:
            e2s[to] = own[:, low:high].astype(bf16)
        else:
            e2s[to] = jnp.zeros((sec, block), bf16)
    each(1, nxy, lambda k: c_e2(k).start())

    each(1, nx, lambda k: c_t1(k).wait_recv())
    tops = [t1s[x, 0:1, :]] + [t1r[k, 0:1, :] for k in range(1, nx)]
    sums = [t1s[x, 1:2, :]] + [t1r[k, 1:2, :] for k in range(1, nx)]
    top = functools.reduce(jnp.maximum, tops)
    factors = [jnp.exp(one - top) for one in tops]
    total = functools.reduce(jnp.add, [a * b for a, b in zip(factors, sums)])
    tr[...] = jnp.zeros_like(tr)
    for n, one in enumerate(list(three_parts(top) + three_parts(total)) + factors):
        tr[n:n + 1, :rows_x] = one
    turned = tr[:, :rows_x].T
    each(1, nx, lambda k: c_a1(k).wait_recv())
    merged = turned[:, 6:7] * a1s[x].astype(f32)
    for k in range(1, nx):
        merged = merged + turned[:, 6 + k:7 + k] * a1r[k].astype(f32)
    a2s[:, :, :lat] = merged.reshape((nz, 2 * per, lat)).astype(bf16)
    a2s[:, :, lat:] = turned.reshape((nz, 2 * per, 128)).astype(bf16)
    each(1, nz, lambda k: c_a2(k).start())

    each(1, nxy, lambda k: c_e2(k).wait_recv())
    summed = e2s[spot].astype(f32)
    for k in range(1, nxy):
        summed = summed + e2r[k].astype(f32)
    e3s[...] = summed.astype(bf16)
    each(1, nz, lambda k: c_e3(k).start())

    first_row = jnp.where(s == 0, ny * 16, 0)
    owner_lane = jnp.where(iota((16, 128), 1) == 0, 1.0, 0.0).astype(bf16)

    def owner_row(count, split):
        row = iota((count, nd * 16), 0)
        source = first_row + 4 * (row // split) + 2
        pull = jnp.where(iota((count, nd * 16), 1) == source, 1.0, 0.0).astype(bf16)
        return dot_rows(owner_lane, dot(pull, notes).astype(bf16))[0:1]

    mine = y.astype(f32)
    out_i, in_i = iota((2 * ny, sec), 0), iota((2 * ny, sec), 1)
    mix_pick = (out_i // 2 == in_i // 4) & (lax.rem(out_i, 2) == lax.rem(in_i, 2))
    mix_pick = jnp.where(mix_pick & (owner_row(sec, 1) == mine), 1.0, 0.0).astype(bf16)
    out_i, in_i = iota((2 * per // 2 * ny, 2 * per * ny), 0), iota((2 * per // 2 * ny, 2 * per * ny), 1)
    attn_pick = (out_i // per == in_i // (2 * per)) & (lax.rem(out_i, per) == lax.rem(in_i, per))
    attn_pick = jnp.where(attn_pick & (owner_row(2 * per * ny, hl) == mine), 1.0, 0.0).astype(bf16)

    a2r[0] = a2s[z]
    each(1, nz, lambda k: c_a2(k).wait_recv())
    arrived = a2r[...].astype(f32)
    tops = arrived[:, :, lat:lat + 1] + arrived[:, :, lat + 1:lat + 2] + arrived[:, :, lat + 2:lat + 3]
    sums = arrived[:, :, lat + 3:lat + 4] + arrived[:, :, lat + 4:lat + 5] + arrived[:, :, lat + 5:lat + 6]
    factors = jnp.exp(tops - jnp.max(tops, axis=0, keepdims=True))
    total = jnp.sum(factors * sums, axis=0)
    a3s[...] = (jnp.sum(factors * arrived[:, :, :lat], axis=0) / total).astype(bf16)
    each(0, ny, lambda k: c_a3(k).start())

    each(1, nz, lambda k: c_e3(k).wait_recv())
    summed = e3s[...].astype(f32)
    for k in range(1, nz):
        summed = summed + e3r[k].astype(f32)
    e5[spot] = summed.astype(bf16)
    each(1, nxy, lambda k: c_e5(k).start())

    each(0, ny, lambda k: c_a3(k).wait_recv())
    finished = a3r[...].astype(f32).reshape((ny * 2 * per, lat)).astype(bf16)
    attn_o[...] = dot(attn_pick, finished).astype(bf16)

    each(1, nd, lambda k: c_e0(k).wait_send())
    each(1, nx, lambda k: c_t1(k).wait_send())
    each(1, nx, lambda k: c_a1(k).wait_send())
    each(1, nz, lambda k: c_a2(k).wait_send())
    each(0, ny, lambda k: c_a3(k).wait_send())
    each(1, 2, lambda k: c_e1(k).wait_send())
    each(1, nxy, lambda k: c_e2(k).wait_send())
    each(1, nz, lambda k: c_e3(k).wait_send())

    each(1, nxy, lambda k: c_e5(k).wait_recv())
    for k in range(nxy):
        low, high = k * block, min((k + 1) * block, width)
        if low < width:
            mix_o[:, low:high] = dot(mix_pick, e5[k]).astype(bf16)
    each(1, nxy, lambda k: c_e5(k).wait_send())


def shards(
    cache_values, cache_rope, cache_scales, queries, new_keys, hidden_rows,
    expert_ids, expert_gates, owners, lengths, up_weight, down_weight,
):
    ny = lax.axis_size("dp")
    nd = ny * lax.axis_size("segment")
    nx = x_chips
    nz = lax.axis_size("ep") // nx
    cv, cr, cs, q = cache_values[0, 0], cache_rope[0, 0], cache_scales[0, 0], queries[0, 0]
    nk, xr, ids, gates = new_keys[0, 0], hidden_rows[0, 0], expert_ids[0, 0], expert_gates[0, 0]
    ctx, lat = cv.shape[1:]
    cols = q.shape[2]
    heads = cols // 2
    hl = heads // (nz * nx)
    width = up_weight.shape[1]
    nxy = nx * ny
    block = -(-width // (nxy * 128)) * 128
    sec = ny * 4
    rows_x = nz * 4 * hl
    vmem = pl.BlockSpec(memory_space=pltpu.VMEM)
    smem = pl.BlockSpec(memory_space=pltpu.SMEM)
    anywhere = pl.BlockSpec(memory_space=pl.ANY)
    sems = lambda n: pltpu.SemaphoreType.DMA((n,))
    attention, mix = pl.pallas_call(
        functools.partial(kernel, (nd, ny, nz, nx)),
        out_shape=(
            jax.ShapeDtypeStruct((ny * 2 * hl, lat), bf16),
            jax.ShapeDtypeStruct((ny * 2, width), bf16),
        ),
        in_specs=[anywhere] * 4 + [vmem] * 6 + [smem] * 2,
        out_specs=(vmem, vmem),
        scratch_shapes=[
            pltpu.VMEM(cv.shape, bf16),
            pltpu.VMEM(q.shape, bf16),
            pltpu.VMEM(up_weight.shape, bf16),
            pltpu.VMEM(down_weight.shape, bf16),
            pltpu.VMEM((128, 128), f32),
            pltpu.VMEM((32, nk.shape[2]), f32),
            pltpu.VMEM((16, width // 4 + 128), f32),
            pltpu.VMEM((nd, 16, width // 4 + 128), bf16),
            pltpu.VMEM((nx, rows_x, lat), bf16),
            pltpu.VMEM((nx, rows_x, lat), bf16),
            pltpu.VMEM((nx, 8, rows_x), f32),
            pltpu.VMEM((nx, 8, rows_x), f32),
            pltpu.VMEM((nz, 4 * hl, lat + 128), bf16),
            pltpu.VMEM((nz, 4 * hl, lat + 128), bf16),
            pltpu.VMEM((4 * hl, lat), bf16),
            pltpu.VMEM((ny, 4 * hl, lat), bf16),
            pltpu.VMEM((sec, width), bf16),
            pltpu.VMEM((sec, width), bf16),
            pltpu.VMEM((nxy, sec, block), bf16),
            pltpu.VMEM((nxy, sec, block), bf16),
            pltpu.VMEM((sec, block), bf16),
            pltpu.VMEM((nz, sec, block), bf16),
            pltpu.VMEM((nxy, sec, block), bf16),
            sems(4),
            sems(nd), sems(nd), sems(nx), sems(nx), sems(nx), sems(nx), sems(nz), sems(nz),
            sems(ny), sems(ny),
            sems(2), sems(2), sems(nxy), sems(nxy), sems(nz), sems(nz), sems(nxy), sems(nxy),
        ],
        compiler_params=pltpu.CompilerParams(
            collective_id=0, has_side_effects=True, vmem_limit_bytes=60 * 1024 * 1024
        ),
    )(cv, q, up_weight, down_weight, cr, cs, nk, xr, ids, gates, owners[0, 0], lengths[0, 0])
    return (
        attention.reshape((1, 1, ny, 2, hl, lat)),
        mix.reshape((1, 1, ny, 2, width)),
    )


def solution(mesh):
    placed = (
        P("segment", "dp", None, "ep", None),
        P("segment", "dp", None, None, "ep"),
        P("segment", "dp", None, None, "ep"),
        P("segment", "dp", None, None, None),
        P("segment", "dp", None, None, None),
        P("segment", "dp", None, None, None),
        P("segment", "dp", None, None, None),
        P("segment", "dp", None, None, None),
        P("segment", "dp", None),
        P("segment", "dp", None),
        P("ep", None, ("segment", "dp")),
        P("ep", ("segment", "dp"), None),
    )
    return jax.shard_map(
        shards,
        mesh=mesh,
        in_specs=placed,
        out_specs=(
            P("segment", "dp", None, None, "ep", None),
            P("segment", "dp", None, None, None),
        ),
        check_vma=False,
    )
```

```python
import functools

import jax
import jax.numpy as jnp
from jax import lax
from jax.experimental import pallas as pl
from jax.experimental.pallas import tpu as pltpu
from jax.sharding import PartitionSpec as P

score_scale = 192.0 ** (-0.5)
far_below = -1e30
x_chips = 4
MESH = pl.DeviceIdType.MESH
f32 = jnp.float32
bf16 = jnp.bfloat16


def iota(shape, dim):
    return lax.broadcasted_iota(jnp.int32, shape, dim)


def dot(a, b):
    return jnp.dot(a, b, preferred_element_type=f32)


def dot_rows(a, b):
    return lax.dot_general(a, b, (((1,), (1,)), ((), ())), preferred_element_type=f32)


def dot_cols(a, b):
    return lax.dot_general(a, b, (((0,), (0,)), ((), ())), preferred_element_type=f32)


def three_parts(value):
    high = value.astype(bf16).astype(f32)
    rest = value - high
    middle = rest.astype(bf16).astype(f32)
    low = (rest - middle).astype(bf16).astype(f32)
    return high, middle, low


def kernel(
    sizes,
    cv_h, q_h, up_h, dn_h, cr_h, cs_h, nk_h, xr_h, ids_h, gates_h, owners_h, lengths_h,
    attn_o, mix_o,
    cv, q, up, dn, cr, cs, nk, xr, ids, gates, owners, lengths, tr, nkp, xf, xg,
    a1s, a1r, t1s, t1r, a2s, a2r, a3s, a3r,
    e1s, e1r, e2s, e2r, e3s, e3r, e5,
    in_sem,
    e0_ss, e0_rs, a1_ss, a1_rs, t1_ss, t1_rs, a2_ss, a2_rs, a3_ss, a3_rs,
    e1_ss, e1_rs, e2_ss, e2_rs, e3_ss, e3_rs, e5_ss, e5_rs,
):
    nd, ny, nz, nx = sizes
    s, y, ep = lax.axis_index("segment"), lax.axis_index("dp"), lax.axis_index("ep")
    z, x = ep // nx, lax.rem(ep, nx)
    d = s * ny + y
    ctx, lat = cv.shape[1], cv.shape[2]
    cols = q.shape[2]
    heads = cols // 2
    hl = heads // (nz * nx)
    width = up.shape[1]
    quarter = width // 4
    pair, side, pairs = z // 2, lax.rem(z, 2), nz // 2
    corner = x * 2 + side
    corners = nx * 2
    spot = y * corners + corner
    spots = ny * corners
    block = e2s.shape[2]
    rows_x = a1s.shape[1]
    sec = ny * 4

    def plane(k):
        to = lax.rem(d + k, nd)
        return to, {"segment": to // ny, "dp": lax.rem(to, ny)}

    def near(k):
        to_x = lax.rem(x + k // 2, nx)
        to_side = lax.rem(side + k % 2, 2)
        return to_x * 2 + to_side, {"ep": (pair * 2 + to_side) * nx + to_x}

    def both_planes(k):
        to_y = lax.rem(y + k // corners, ny)
        to_x = lax.rem(x + (k // 2) % nx, nx)
        to_side = lax.rem(side + k % 2, 2)
        return (to_y * nx + to_x) * 2 + to_side, {
            "dp": to_y, "ep": (pair * 2 + to_side) * nx + to_x,
        }

    def far(k):
        to = lax.rem(pair + k, pairs)
        return to, {"ep": (to * 2 + side) * nx + x}

    def across(k):
        to = lax.rem(y + k, ny)
        return to, {"segment": 1 - s, "dp": to}

    def remote(src, dst, ss, rs, k, to):
        return pltpu.make_async_remote_copy(
            src_ref=src, dst_ref=dst, send_sem=ss.at[k], recv_sem=rs.at[k],
            device_id=to, device_id_type=MESH,
        )

    def c_e0(k):
        return remote(xg.at[d], xg.at[d], e0_ss, e0_rs, k, plane(k)[1])

    def c_a1(k):
        to, dev = near(k)
        return remote(a1s.at[to], a1r.at[k], a1_ss, a1_rs, k, dev)

    def c_t1(k):
        to, dev = near(k)
        return remote(t1s.at[to], t1r.at[k], t1_ss, t1_rs, k, dev)

    def c_a2(k):
        to, dev = far(k)
        return remote(a2s.at[to], a2r.at[k], a2_ss, a2_rs, k, dev)

    def c_a3(k):
        return remote(a3s, a3r.at[y], a3_ss, a3_rs, k, across(k)[1])

    def c_e1(k):
        return remote(e1s, e1r, e1_ss, e1_rs, k, {"segment": 1 - s})

    def c_e2(k):
        to, dev = both_planes(k)
        return remote(e2s.at[to], e2r.at[k], e2_ss, e2_rs, k, dev)

    def c_e3(k):
        return remote(e3s, e3r.at[k], e3_ss, e3_rs, k, far(k)[1])

    def c_e5(k):
        return remote(e5.at[spot], e5.at[spot], e5_ss, e5_rs, k, both_planes(k)[1])

    def each(first, last, act):
        for k in range(first, last):
            act(k)

    barrier = pltpu.get_barrier_semaphore()

    def greet(where):
        def act(k):
            pl.semaphore_signal(barrier, inc=1, device_id=where(k)[1], device_id_type=MESH)

        return act

    each(1, pairs, greet(far))
    each(1, nd, greet(plane))
    for k in range(1, spots):
        if k % corners:
            greet(both_planes)(k)

    loads = {}
    for n, (name, src, dst) in enumerate((
        ("rows", xr_h, xr), ("ids", ids_h, ids), ("gates", gates_h, gates), ("owners", owners_h, owners),
        ("values", cv_h, cv), ("scales", cs_h, cs), ("queries", q_h, q), ("rope", cr_h, cr),
        ("fresh", nk_h, nk), ("lengths", lengths_h, lengths), ("up", up_h, up), ("down", dn_h, dn),
    )):
        loads[name] = pltpu.make_async_copy(src, dst, in_sem.at[n])
        loads[name].start()

    xf[...] = jnp.zeros_like(xf)
    for name in ("rows", "ids", "gates", "owners"):
        loads[name].wait()
    for r in range(2):
        for j in range(2):
            i = 2 * r + j
            row = xr[r, j:j + 1, :].astype(f32)
            for part in range(4):
                xf[4 * i + part:4 * i + part + 1, :quarter] = row[:, part * quarter:(part + 1) * quarter]
            xf[4 * i:4 * i + 1, quarter:quarter + 8] = ids[r, j:j + 1, :].astype(f32)
            xf[4 * i + 1:4 * i + 2, quarter:quarter + 8] = gates[r, j:j + 1, :].astype(f32)
            xf[4 * i + 2:4 * i + 3, quarter:] = jnp.full((1, 128), owners[r], jnp.int32).astype(f32)
    xg[d] = xf[...].astype(bf16)

    tr[...] = jnp.zeros_like(tr)
    nkp[...] = jnp.zeros_like(nkp)
    loads["scales"].wait()
    loads["fresh"].wait()
    for r in range(2):
        tr[8 * r:8 * r + 4, :ctx] = cs[r].astype(f32)
        nkp[16 * r:16 * r + 2, :] = nk[r].astype(f32)
    scale_cols = tr[:, :ctx].T
    total_rows = corners * rows_x
    place = iota((total_rows, cols), 0)
    per = 2 * hl
    h_of = lax.rem(place, hl)
    j_of = lax.rem(place // hl, 2)
    r_of = lax.rem(place // per, 2)
    pair_of = lax.rem(place // (2 * per), pairs)
    side_of = lax.rem(place // (2 * per * pairs), 2)
    x_of = place // (4 * per * pairs)
    z_of = pair_of * 2 + side_of
    match = (j_of * heads + (z_of * nx + x_of) * hl + h_of) == iota((total_rows, cols), 1)
    for name in ("values", "queries", "rope", "lengths"):
        loads[name].wait()
    out = jnp.zeros((total_rows, lat), f32)
    stats = jnp.zeros((16, total_rows), f32)
    for r in range(2):
        latent = jnp.concatenate(
            [
                cv[r, :, b * 128:(b + 1) * 128].astype(f32) * scale_cols[:, 8 * r + b:8 * r + b + 1]
                for b in range(lat // 128)
            ],
            axis=1,
        ).astype(bf16)
        fresh = nkp[16 * r:16 * r + 16, :].astype(bf16)
        cached = dot(latent, q[r, :lat, :]) + dot_cols(cr[r], q[r, lat:, :])
        newer = dot(fresh[:, :lat], q[r, :lat, :]) + dot(fresh[:, lat:], q[r, lat:, :])
        cached_ok = ep * ctx + iota((ctx, cols), 0) < lengths[r]
        newer_ok = (iota((16, cols), 0) + jnp.where(ep == 0, 0, 16)) <= (iota((16, cols), 1) // heads)
        cached = jnp.where(cached_ok, cached * score_scale, far_below)
        newer = jnp.where(newer_ok, newer * score_scale, far_below)
        peak = jnp.maximum(
            jnp.max(cached, axis=0, keepdims=True), jnp.max(newer, axis=0, keepdims=True)
        )
        cached = jnp.where(cached_ok, jnp.exp(cached - peak), 0.0)
        newer = jnp.where(newer_ok, jnp.exp(newer - peak), 0.0)
        total = jnp.sum(cached, axis=0, keepdims=True) + jnp.sum(newer, axis=0, keepdims=True)
        line = iota((16, cols), 0)
        extra = jnp.zeros((16, cols), f32)
        for n, part in enumerate(three_parts(peak) + three_parts(total)):
            extra = jnp.where(line == n, part, extra)
        order = jnp.where(match & (r_of == r), 1.0, 0.0).astype(bf16)
        out = out + dot(dot_rows(order, cached.astype(bf16)).astype(bf16), latent)
        out = out + dot(dot_rows(order, newer.astype(bf16)).astype(bf16), fresh[:, :lat])
        stats = stats + dot_rows(extra.astype(bf16), order)
    t1s[...] = jnp.zeros_like(t1s)
    peak = stats[0:1] + stats[1:2] + stats[2:3]
    total = stats[3:4] + stats[4:5] + stats[5:6]
    for to in range(corners):
        a1s[to] = out[to * rows_x:(to + 1) * rows_x].astype(bf16)
        t1s[to, 0:1, :rows_x] = peak[:, to * rows_x:(to + 1) * rows_x]
        t1s[to, 1:2, :rows_x] = total[:, to * rows_x:(to + 1) * rows_x]
    pl.semaphore_wait(barrier, (pairs - 1) + (nd - 1) + (spots - ny))
    each(1, nd, lambda k: c_e0(k).start())
    each(1, corners, lambda k: c_t1(k).start())
    each(1, corners, lambda k: c_a1(k).start())

    row_count = nd * 4
    want = iota((3 * row_count, nd * 16), 0)
    pick = iota((3 * row_count, nd * 16), 1) == 4 * lax.rem(want, row_count) + want // row_count
    pick = jnp.where(pick, 1.0, 0.0).astype(bf16)
    lane = iota((row_count, 128), 1)
    experts, hidden_width = up.shape[0], up.shape[2]
    part_of = lax.rem(iota((nd * 16, experts * hidden_width), 0), 4)
    loads["up"].wait()
    loads["down"].wait()
    each(1, nd, lambda k: c_e0(k).wait_recv())
    gathered = xg[...].reshape((nd * 16, xg.shape[2]))
    acc = jnp.zeros((nd * 16, experts * hidden_width), f32)
    for part in range(4):
        weights = jnp.concatenate(
            [up[e, part * quarter:(part + 1) * quarter, :] for e in range(experts)], axis=1
        )
        acc = jnp.where(part_of == part, dot(gathered[:, :quarter], weights), acc)
    notes = gathered[:, quarter:]
    routing = dot(pick, notes)
    chosen, gate_values = routing[:row_count], routing[row_count:2 * row_count]
    acc = acc + pltpu.roll(acc, nd * 16 - 1, 0)
    acc = acc + pltpu.roll(acc, nd * 16 - 2, 0)
    hidden = (acc / (1.0 + jnp.exp(-acc))).astype(bf16)
    hidden = dot(pick[:row_count], hidden).astype(bf16)
    partial = jnp.zeros((row_count, width), f32)
    for e in range(experts):
        expert = (ep * experts + e).astype(f32)
        gate = jnp.sum(
            jnp.where((chosen == expert) & (lane < 8), gate_values, 0.0), axis=1, keepdims=True
        )
        partial = partial + gate * dot(hidden[:, e * hidden_width:(e + 1) * hidden_width], dn[e])
    first, second = partial[:sec], partial[sec:]
    e1s[...] = jnp.where(s == 0, first, second).astype(bf16)
    each(1, 2, lambda k: c_e1(k).start())
    own = jnp.where(s == 0, second, first)

    each(1, 2, lambda k: c_e1(k).wait_recv())
    own = own + e1r[...].astype(f32)
    for to in range(spots):
        low, high = to * block, min((to + 1) * block, width)
        if low < width:
            e2s[to] = own[:, low:high].astype(bf16)
        else:
            e2s[to] = jnp.zeros((sec, block), bf16)
    each(1, spots, lambda k: c_e2(k).start())

    each(1, corners, lambda k: c_t1(k).wait_recv())
    tops = [t1s[corner, 0:1, :rows_x]] + [t1r[k, 0:1, :rows_x] for k in range(1, corners)]
    sums = [t1s[corner, 1:2, :rows_x]] + [t1r[k, 1:2, :rows_x] for k in range(1, corners)]
    top = functools.reduce(jnp.maximum, tops)
    factors = [jnp.exp(one - top) for one in tops]
    total = functools.reduce(jnp.add, [a * b for a, b in zip(factors, sums)])
    tr[...] = jnp.zeros_like(tr)
    for n, one in enumerate(list(three_parts(top) + three_parts(total)) + factors):
        tr[n:n + 1, :rows_x] = one
    turned = tr[...].T[:rows_x]
    each(1, corners, lambda k: c_a1(k).wait_recv())
    merged = turned[:, 6:7] * a1s[corner].astype(f32)
    for k in range(1, corners):
        merged = merged + turned[:, 6 + k:7 + k] * a1r[k].astype(f32)
    a2s[:, :, :lat] = merged.reshape((pairs, 2 * per, lat)).astype(bf16)
    a2s[:, :, lat:] = turned.reshape((pairs, 2 * per, 128)).astype(bf16)
    each(1, pairs, lambda k: c_a2(k).start())

    each(1, spots, lambda k: c_e2(k).wait_recv())
    summed = e2s[spot].astype(f32)
    for k in range(1, spots):
        summed = summed + e2r[k].astype(f32)
    e3s[...] = summed.astype(bf16)
    each(1, pairs, lambda k: c_e3(k).start())

    first_row = jnp.where(s == 0, ny * 16, 0)
    owner_lane = jnp.where(iota((16, 128), 1) == 0, 1.0, 0.0).astype(bf16)

    def owner_row(count, split):
        row = iota((count, nd * 16), 0)
        source = first_row + 4 * (row // split) + 2
        pull = jnp.where(iota((count, nd * 16), 1) == source, 1.0, 0.0).astype(bf16)
        return dot_rows(owner_lane, dot(pull, notes).astype(bf16))[0:1]

    mine = y.astype(f32)
    out_i, in_i = iota((2 * ny, sec), 0), iota((2 * ny, sec), 1)
    mix_pick = (out_i // 2 == in_i // 4) & (lax.rem(out_i, 2) == lax.rem(in_i, 2))
    mix_pick = jnp.where(mix_pick & (owner_row(sec, 1) == mine), 1.0, 0.0).astype(bf16)
    out_i, in_i = iota((2 * per // 2 * ny, 2 * per * ny), 0), iota((2 * per // 2 * ny, 2 * per * ny), 1)
    attn_pick = (out_i // per == in_i // (2 * per)) & (lax.rem(out_i, per) == lax.rem(in_i, per))
    attn_pick = jnp.where(attn_pick & (owner_row(2 * per * ny, hl) == mine), 1.0, 0.0).astype(bf16)

    a2r[0] = a2s[pair]
    each(1, pairs, lambda k: c_a2(k).wait_recv())
    arrived = a2r[...].astype(f32)
    tops = arrived[:, :, lat:lat + 1] + arrived[:, :, lat + 1:lat + 2] + arrived[:, :, lat + 2:lat + 3]
    sums = arrived[:, :, lat + 3:lat + 4] + arrived[:, :, lat + 4:lat + 5] + arrived[:, :, lat + 5:lat + 6]
    factors = jnp.exp(tops - jnp.max(tops, axis=0, keepdims=True))
    total = jnp.sum(factors * sums, axis=0)
    a3s[...] = (jnp.sum(factors * arrived[:, :, :lat], axis=0) / total).astype(bf16)
    each(0, ny, lambda k: c_a3(k).start())

    each(1, pairs, lambda k: c_e3(k).wait_recv())
    summed = e3s[...].astype(f32)
    for k in range(1, pairs):
        summed = summed + e3r[k].astype(f32)
    e5[spot] = summed.astype(bf16)
    each(1, spots, lambda k: c_e5(k).start())

    each(0, ny, lambda k: c_a3(k).wait_recv())
    finished = a3r[...].astype(f32).reshape((ny * 2 * per, lat)).astype(bf16)
    attn_o[...] = dot(attn_pick, finished).astype(bf16)

    each(1, nd, lambda k: c_e0(k).wait_send())
    each(1, corners, lambda k: c_t1(k).wait_send())
    each(1, corners, lambda k: c_a1(k).wait_send())
    each(1, pairs, lambda k: c_a2(k).wait_send())
    each(0, ny, lambda k: c_a3(k).wait_send())
    each(1, 2, lambda k: c_e1(k).wait_send())
    each(1, spots, lambda k: c_e2(k).wait_send())
    each(1, pairs, lambda k: c_e3(k).wait_send())

    each(1, spots, lambda k: c_e5(k).wait_recv())
    for k in range(spots):
        low, high = k * block, min((k + 1) * block, width)
        if low < width:
            mix_o[:, low:high] = dot(mix_pick, e5[k]).astype(bf16)
    each(1, spots, lambda k: c_e5(k).wait_send())


def shards(
    cache_values, cache_rope, cache_scales, queries, new_keys, hidden_rows,
    expert_ids, expert_gates, owners, lengths, up_weight, down_weight,
):
    ny = lax.axis_size("dp")
    nd = ny * lax.axis_size("segment")
    nx = x_chips
    nz = lax.axis_size("ep") // nx
    cv, cr, cs, q = cache_values[0, 0], cache_rope[0, 0], cache_scales[0, 0], queries[0, 0]
    nk, xr, ids, gates = new_keys[0, 0], hidden_rows[0, 0], expert_ids[0, 0], expert_gates[0, 0]
    ctx, lat = cv.shape[1:]
    cols = q.shape[2]
    heads = cols // 2
    hl = heads // (nz * nx)
    width = up_weight.shape[1]
    corners, pairs = nx * 2, nz // 2
    spots = ny * corners
    block = -(-width // (spots * 128)) * 128
    sec = ny * 4
    rows_x = pairs * 4 * hl
    vmem = pl.BlockSpec(memory_space=pltpu.VMEM)
    anywhere = pl.BlockSpec(memory_space=pl.ANY)
    sems = lambda n: pltpu.SemaphoreType.DMA((n,))
    attention, mix = pl.pallas_call(
        functools.partial(kernel, (nd, ny, nz, nx)),
        out_shape=(
            jax.ShapeDtypeStruct((ny * 2 * hl, lat), bf16),
            jax.ShapeDtypeStruct((ny * 2, width), bf16),
        ),
        in_specs=[anywhere] * 12,
        out_specs=(vmem, vmem),
        scratch_shapes=[
            pltpu.VMEM(cv.shape, bf16),
            pltpu.VMEM(q.shape, bf16),
            pltpu.VMEM(up_weight.shape, bf16),
            pltpu.VMEM(down_weight.shape, bf16),
            pltpu.VMEM(cr.shape, bf16),
            pltpu.VMEM(cs.shape, bf16),
            pltpu.VMEM(nk.shape, bf16),
            pltpu.VMEM(xr.shape, bf16),
            pltpu.VMEM(ids.shape, jnp.int32),
            pltpu.VMEM(gates.shape, bf16),
            pltpu.SMEM(owners[0, 0].shape, jnp.int32),
            pltpu.SMEM(lengths[0, 0].shape, jnp.int32),
            pltpu.VMEM((128, 128), f32),
            pltpu.VMEM((32, nk.shape[2]), f32),
            pltpu.VMEM((16, width // 4 + 128), f32),
            pltpu.VMEM((nd, 16, width // 4 + 128), bf16),
            pltpu.VMEM((corners, rows_x, lat), bf16),
            pltpu.VMEM((corners, rows_x, lat), bf16),
            pltpu.VMEM((corners, 8, 128), f32),
            pltpu.VMEM((corners, 8, 128), f32),
            pltpu.VMEM((pairs, 4 * hl, lat + 128), bf16),
            pltpu.VMEM((pairs, 4 * hl, lat + 128), bf16),
            pltpu.VMEM((4 * hl, lat), bf16),
            pltpu.VMEM((ny, 4 * hl, lat), bf16),
            pltpu.VMEM((sec, width), bf16),
            pltpu.VMEM((sec, width), bf16),
            pltpu.VMEM((spots, sec, block), bf16),
            pltpu.VMEM((spots, sec, block), bf16),
            pltpu.VMEM((sec, block), bf16),
            pltpu.VMEM((pairs, sec, block), bf16),
            pltpu.VMEM((spots, sec, block), bf16),
            sems(12),
            sems(nd), sems(nd), sems(corners), sems(corners), sems(corners), sems(corners),
            sems(pairs), sems(pairs), sems(ny), sems(ny),
            sems(2), sems(2), sems(spots), sems(spots), sems(pairs), sems(pairs), sems(spots), sems(spots),
        ],
        compiler_params=pltpu.CompilerParams(
            collective_id=0, has_side_effects=True, vmem_limit_bytes=60 * 1024 * 1024
        ),
    )(cv, q, up_weight, down_weight, cr, cs, nk, xr, ids, gates, owners[0, 0], lengths[0, 0])
    return (
        attention.reshape((1, 1, ny, 2, hl, lat)),
        mix.reshape((1, 1, ny, 2, width)),
    )


def solution(mesh):
    placed = (
        P("segment", "dp", None, "ep", None),
        P("segment", "dp", None, None, "ep"),
        P("segment", "dp", None, None, "ep"),
        P("segment", "dp", None, None, None),
        P("segment", "dp", None, None, None),
        P("segment", "dp", None, None, None),
        P("segment", "dp", None, None, None),
        P("segment", "dp", None, None, None),
        P("segment", "dp", None),
        P("segment", "dp", None),
        P("ep", None, ("segment", "dp")),
        P("ep", ("segment", "dp"), None),
    )
    return jax.shard_map(
        shards,
        mesh=mesh,
        in_specs=placed,
        out_specs=(
            P("segment", "dp", None, None, "ep", None),
            P("segment", "dp", None, None, None),
        ),
        check_vma=False,
    )
```

```python
import functools

import jax
import jax.numpy as jnp
from jax import lax
from jax.experimental import pallas as pl
from jax.experimental.pallas import tpu as pltpu
from jax.sharding import PartitionSpec as P

score_scale = 192.0 ** (-0.5)
far_below = -1e30
x_chips = 4
MESH = pl.DeviceIdType.MESH
f32 = jnp.float32
bf16 = jnp.bfloat16


def iota(shape, dim):
    return lax.broadcasted_iota(jnp.int32, shape, dim)


def dot(a, b):
    return jnp.dot(a, b, preferred_element_type=f32)


def dot_rows(a, b):
    return lax.dot_general(a, b, (((1,), (1,)), ((), ())), preferred_element_type=f32)


def dot_cols(a, b):
    return lax.dot_general(a, b, (((0,), (0,)), ((), ())), preferred_element_type=f32)


def three_parts(value):
    high = value.astype(bf16).astype(f32)
    rest = value - high
    middle = rest.astype(bf16).astype(f32)
    low = (rest - middle).astype(bf16).astype(f32)
    return high, middle, low


def kernel(
    sizes,
    cv_h, q_h, up_h, dn_h, cr_h, cs_h, nk_h, xr_h, ids_h, gates_h, owners_h, lengths_h,
    attn_o, mix_o,
    cv, q, up, dn, cr, cs, nk, xr, ids, gates, owners, lengths, tr, nkp, xf, xg,
    a1s, a1r, t1s, t1r, a2s, a2r, a3s, a3r,
    e1s, e1r, e2s, e2r, e3s, e3r, e5,
    in_sem,
    e0_ss, e0_rs, a1_ss, a1_rs, t1_ss, t1_rs, a2_ss, a2_rs, a3_ss, a3_rs,
    e1_ss, e1_rs, e2_ss, e2_rs, e3_ss, e3_rs, e5_ss, e5_rs,
):
    nd, ny, nz, nx = sizes
    s, y, ep = lax.axis_index("segment"), lax.axis_index("dp"), lax.axis_index("ep")
    z, x = ep // nx, lax.rem(ep, nx)
    d = s * ny + y
    ctx, lat = cv.shape[1], cv.shape[2]
    cols = q.shape[2]
    heads = cols // 2
    hl = heads // (nz * nx)
    width = up.shape[1]
    quarter = width // 4
    pair, side, pairs = z // 2, lax.rem(z, 2), nz // 2
    corner = x * 2 + side
    corners = nx * 2
    spot = y * corners + corner
    spots = ny * corners
    block = e2s.shape[3]
    strip = corners * block
    rows_x = a1s.shape[1]
    sec = ny * 4

    def plane(k):
        to = lax.rem(d + k, nd)
        return to, {"segment": to // ny, "dp": lax.rem(to, ny)}

    def near(k):
        to_x = lax.rem(x + k // 2, nx)
        to_side = lax.rem(side + k % 2, 2)
        return to_x * 2 + to_side, {"ep": (pair * 2 + to_side) * nx + to_x}

    def both_planes(k):
        to_y = lax.rem(y + k // corners, ny)
        to_x = lax.rem(x + (k // 2) % nx, nx)
        to_side = lax.rem(side + k % 2, 2)
        return (to_y * nx + to_x) * 2 + to_side, {
            "dp": to_y, "ep": (pair * 2 + to_side) * nx + to_x,
        }

    def far(k):
        to = lax.rem(pair + k, pairs)
        return to, {"ep": (to * 2 + side) * nx + x}

    def across(k):
        to = lax.rem(y + k, ny)
        return to, {"segment": 1 - s, "dp": to}

    def remote(src, dst, ss, rs, k, to):
        return pltpu.make_async_remote_copy(
            src_ref=src, dst_ref=dst, send_sem=ss.at[k], recv_sem=rs.at[k],
            device_id=to, device_id_type=MESH,
        )

    def c_e0(k):
        return remote(xg.at[d], xg.at[d], e0_ss, e0_rs, k, plane(k)[1])

    def c_a1(k):
        to, dev = near(k)
        return remote(a1s.at[to], a1r.at[k], a1_ss, a1_rs, k, dev)

    def c_t1(k):
        to, dev = near(k)
        return remote(t1s.at[to], t1r.at[k], t1_ss, t1_rs, k, dev)

    def c_a2(k):
        to, dev = far(k)
        return remote(a2s.at[to], a2r.at[k], a2_ss, a2_rs, k, dev)

    def c_a3(k):
        return remote(a3s, a3r.at[y], a3_ss, a3_rs, k, across(k)[1])

    def c_e1(k):
        return remote(e1s.at[k], e1r.at[k], e1_ss, e1_rs, k, {"segment": 1 - s})

    def c_e2(k):
        to, dev = both_planes(k)
        return remote(e2s.at[k // corners, lax.rem(to, corners)], e2r.at[k], e2_ss, e2_rs, k, dev)

    def c_e3(k):
        return remote(e3s, e3r.at[k], e3_ss, e3_rs, k, far(k)[1])

    def c_e5(k):
        return remote(e5.at[spot], e5.at[spot], e5_ss, e5_rs, k, both_planes(k)[1])

    def each(first, last, act):
        for k in range(first, last):
            act(k)

    def ring(k, n):
        return min(k % n, -k % n)

    def farthest(first, last, hops):
        return sorted(range(first, last), key=lambda k: -hops(k))

    plane_order = farthest(1, nd, lambda k: ring(k, ny) if k % ny else 0.5)
    near_order = farthest(1, corners, lambda k: ring(k // 2, nx) + k % 2)
    far_order = farthest(1, pairs, lambda k: ring(k, pairs))
    strips = farthest(0, ny, lambda k: ring(k, ny))
    corner_order = farthest(0, corners, lambda k: ring(k // 2, nx) + k % 2)
    spot_order = farthest(
        1, spots, lambda k: ring(k // corners, ny) + ring((k % corners) // 2, nx) + k % 2
    )

    def start(copy, order):
        for k in order:
            copy(k).start()

    barrier = pltpu.get_barrier_semaphore()

    def greet(where):
        def act(k):
            pl.semaphore_signal(barrier, inc=1, device_id=where(k)[1], device_id_type=MESH)

        return act

    each(1, nd, greet(plane))
    each(1, pairs, greet(far))
    for k in range(1, spots):
        if k % corners:
            greet(both_planes)(k)

    loads = {}
    for n, (name, src, dst) in enumerate((
        ("rows", xr_h, xr), ("ids", ids_h, ids), ("gates", gates_h, gates), ("owners", owners_h, owners),
        ("values", cv_h, cv), ("scales", cs_h, cs), ("queries", q_h, q), ("rope", cr_h, cr),
        ("fresh", nk_h, nk), ("lengths", lengths_h, lengths), ("up", up_h, up), ("down", dn_h, dn.at[:, :, :width]),
    )):
        loads[name] = pltpu.make_async_copy(src, dst, in_sem.at[n])
        loads[name].start()

    xf[...] = jnp.zeros_like(xf)
    for name in ("rows", "ids", "gates", "owners"):
        loads[name].wait()
    for r in range(2):
        for j in range(2):
            i = 2 * r + j
            row = xr[r, j:j + 1, :].astype(f32)
            for part in range(4):
                xf[4 * i + part:4 * i + part + 1, :quarter] = row[:, part * quarter:(part + 1) * quarter]
            xf[4 * i:4 * i + 1, quarter:quarter + 8] = ids[r, j:j + 1, :].astype(f32)
            xf[4 * i + 1:4 * i + 2, quarter:quarter + 8] = gates[r, j:j + 1, :].astype(f32)
            xf[4 * i + 2:4 * i + 3, quarter:] = jnp.full((1, 128), owners[r], jnp.int32).astype(f32)
    xg[d] = xf[...].astype(bf16)

    tr[...] = jnp.zeros_like(tr)
    nkp[...] = jnp.zeros_like(nkp)
    loads["scales"].wait()
    loads["fresh"].wait()
    for r in range(2):
        tr[8 * r:8 * r + 4, :ctx] = cs[r].astype(f32)
        nkp[16 * r:16 * r + 2, :] = nk[r].astype(f32)
    scale_cols = tr[:, :ctx].T
    total_rows = corners * rows_x
    place = iota((total_rows, cols), 0)
    per = 2 * hl
    h_of = lax.rem(place, hl)
    j_of = lax.rem(place // hl, 2)
    r_of = lax.rem(place // per, 2)
    pair_of = lax.rem(place // (2 * per), pairs)
    side_of = lax.rem(place // (2 * per * pairs), 2)
    x_of = place // (4 * per * pairs)
    z_of = pair_of * 2 + side_of
    match = (j_of * heads + (z_of * nx + x_of) * hl + h_of) == iota((total_rows, cols), 1)
    for name in ("values", "queries", "rope", "lengths"):
        loads[name].wait()
    out = jnp.zeros((total_rows, lat), f32)
    stats = jnp.zeros((16, total_rows), f32)
    for r in range(2):
        latent = jnp.concatenate(
            [
                cv[r, :, b * 128:(b + 1) * 128].astype(f32) * scale_cols[:, 8 * r + b:8 * r + b + 1]
                for b in range(lat // 128)
            ],
            axis=1,
        ).astype(bf16)
        fresh = nkp[16 * r:16 * r + 16, :].astype(bf16)
        cached = dot(latent, q[r, :lat, :]) + dot_cols(cr[r], q[r, lat:, :])
        newer = dot(fresh[:, :lat], q[r, :lat, :]) + dot(fresh[:, lat:], q[r, lat:, :])
        cached_ok = ep * ctx + iota((ctx, cols), 0) < lengths[r]
        newer_ok = (iota((16, cols), 0) + jnp.where(ep == 0, 0, 16)) <= (iota((16, cols), 1) // heads)
        cached = jnp.where(cached_ok, cached * score_scale, far_below)
        newer = jnp.where(newer_ok, newer * score_scale, far_below)
        peak = jnp.maximum(
            jnp.max(cached, axis=0, keepdims=True), jnp.max(newer, axis=0, keepdims=True)
        )
        cached = jnp.where(cached_ok, jnp.exp(cached - peak), 0.0)
        newer = jnp.where(newer_ok, jnp.exp(newer - peak), 0.0)
        total = jnp.sum(cached, axis=0, keepdims=True) + jnp.sum(newer, axis=0, keepdims=True)
        line = iota((16, cols), 0)
        extra = jnp.zeros((16, cols), f32)
        for n, part in enumerate(three_parts(peak) + three_parts(total)):
            extra = jnp.where(line == n, part, extra)
        order = jnp.where(match & (r_of == r), 1.0, 0.0).astype(bf16)
        out = out + dot(dot_rows(order, cached.astype(bf16)).astype(bf16), latent)
        out = out + dot(dot_rows(order, newer.astype(bf16)).astype(bf16), fresh[:, :lat])
        stats = stats + dot_rows(extra.astype(bf16), order)
    t1s[...] = jnp.zeros_like(t1s)
    peak = stats[0:1] + stats[1:2] + stats[2:3]
    total = stats[3:4] + stats[4:5] + stats[5:6]
    for to in range(corners):
        a1s[to] = out[to * rows_x:(to + 1) * rows_x].astype(bf16)
        t1s[to, 0:1, :rows_x] = peak[:, to * rows_x:(to + 1) * rows_x]
        t1s[to, 1:2, :rows_x] = total[:, to * rows_x:(to + 1) * rows_x]
    pl.semaphore_wait(barrier, (pairs - 1) + (nd - 1) + (spots - ny))
    start(c_e0, plane_order)
    start(c_t1, near_order)
    start(c_a1, near_order)

    row_count = nd * 4
    want = iota((3 * row_count, nd * 16), 0)
    pick = iota((3 * row_count, nd * 16), 1) == 4 * lax.rem(want, row_count) + want // row_count
    pick = jnp.where(pick, 1.0, 0.0).astype(bf16)
    lane = iota((row_count, 128), 1)
    experts, hidden_width = up.shape[0], up.shape[2]
    if dn.shape[2] > width:
        dn[:, :, width:] = jnp.zeros((experts, hidden_width, dn.shape[2] - width), bf16)
    part_of = lax.rem(iota((nd * 16, experts * hidden_width), 0), 4)
    loads["up"].wait()
    loads["down"].wait()
    each(1, nd, lambda k: c_e0(k).wait_recv())
    gathered = xg[...].reshape((nd * 16, xg.shape[2]))
    acc = jnp.zeros((nd * 16, experts * hidden_width), f32)
    for part in range(4):
        weights = jnp.concatenate(
            [up[e, part * quarter:(part + 1) * quarter, :] for e in range(experts)], axis=1
        )
        acc = jnp.where(part_of == part, dot(gathered[:, :quarter], weights), acc)
    notes = gathered[:, quarter:]
    routing = dot(pick, notes)
    chosen, gate_values = routing[:row_count], routing[row_count:2 * row_count]
    acc = acc + pltpu.roll(acc, nd * 16 - 1, 0)
    acc = acc + pltpu.roll(acc, nd * 16 - 2, 0)
    hidden = (acc / (1.0 + jnp.exp(-acc))).astype(bf16)
    hidden = dot(pick[:row_count], hidden).astype(bf16)
    hiddens, expert_gates = [], []
    for e in range(experts):
        expert = (ep * experts + e).astype(f32)
        expert_gates.append(jnp.sum(
            jnp.where((chosen == expert) & (lane < 8), gate_values, 0.0), axis=1, keepdims=True
        ))
        hiddens.append(hidden[:, e * hidden_width:(e + 1) * hidden_width])
    owns = {}
    for j in strips:
        low = pl.multiple_of(lax.rem(y + j, ny) * strip, 128)
        partial = jnp.zeros((row_count, strip), f32)
        for e in range(experts):
            partial = partial + expert_gates[e] * dot(hiddens[e], dn[e, :, pl.ds(low, strip)])
        first, second = partial[:sec], partial[sec:]
        e1s[j] = jnp.where(s == 0, first, second).astype(bf16)
        c_e1(j).start()
        owns[j] = jnp.where(s == 0, second, first)

    for j in strips:
        c_e1(j).wait_recv()
        own = owns[j] + e1r[j].astype(f32)
        for to in range(corners):
            e2s[j, to] = own[:, to * block:(to + 1) * block].astype(bf16)
        start(c_e2, [k for k in (j * corners + c for c in corner_order) if k])

    each(1, corners, lambda k: c_t1(k).wait_recv())
    tops = [t1s[corner, 0:1, :rows_x]] + [t1r[k, 0:1, :rows_x] for k in range(1, corners)]
    sums = [t1s[corner, 1:2, :rows_x]] + [t1r[k, 1:2, :rows_x] for k in range(1, corners)]
    top = functools.reduce(jnp.maximum, tops)
    factors = [jnp.exp(one - top) for one in tops]
    total = functools.reduce(jnp.add, [a * b for a, b in zip(factors, sums)])
    tr[...] = jnp.zeros_like(tr)
    for n, one in enumerate(list(three_parts(top) + three_parts(total)) + factors):
        tr[n:n + 1, :rows_x] = one
    turned = tr[...].T[:rows_x]
    each(1, corners, lambda k: c_a1(k).wait_recv())
    merged = turned[:, 6:7] * a1s[corner].astype(f32)
    for k in range(1, corners):
        merged = merged + turned[:, 6 + k:7 + k] * a1r[k].astype(f32)
    a2s[:, :, :lat] = merged.reshape((pairs, 2 * per, lat)).astype(bf16)
    a2s[:, :, lat:] = turned.reshape((pairs, 2 * per, 128)).astype(bf16)
    start(c_a2, far_order)

    each(1, spots, lambda k: c_e2(k).wait_recv())
    summed = e2s[0, corner].astype(f32)
    for k in range(1, spots):
        summed = summed + e2r[k].astype(f32)
    e3s[...] = summed.astype(bf16)
    start(c_e3, far_order)

    first_row = jnp.where(s == 0, ny * 16, 0)
    owner_lane = jnp.where(iota((16, 128), 1) == 0, 1.0, 0.0).astype(bf16)

    def owner_row(count, split):
        row = iota((count, nd * 16), 0)
        source = first_row + 4 * (row // split) + 2
        pull = jnp.where(iota((count, nd * 16), 1) == source, 1.0, 0.0).astype(bf16)
        return dot_rows(owner_lane, dot(pull, notes).astype(bf16))[0:1]

    mine = y.astype(f32)
    out_i, in_i = iota((2 * ny, sec), 0), iota((2 * ny, sec), 1)
    mix_pick = (out_i // 2 == in_i // 4) & (lax.rem(out_i, 2) == lax.rem(in_i, 2))
    mix_pick = jnp.where(mix_pick & (owner_row(sec, 1) == mine), 1.0, 0.0).astype(bf16)
    out_i, in_i = iota((2 * per // 2 * ny, 2 * per * ny), 0), iota((2 * per // 2 * ny, 2 * per * ny), 1)
    attn_pick = (out_i // per == in_i // (2 * per)) & (lax.rem(out_i, per) == lax.rem(in_i, per))
    attn_pick = jnp.where(attn_pick & (owner_row(2 * per * ny, hl) == mine), 1.0, 0.0).astype(bf16)

    a2r[0] = a2s[pair]
    each(1, pairs, lambda k: c_a2(k).wait_recv())
    arrived = a2r[...].astype(f32)
    tops = arrived[:, :, lat:lat + 1] + arrived[:, :, lat + 1:lat + 2] + arrived[:, :, lat + 2:lat + 3]
    sums = arrived[:, :, lat + 3:lat + 4] + arrived[:, :, lat + 4:lat + 5] + arrived[:, :, lat + 5:lat + 6]
    factors = jnp.exp(tops - jnp.max(tops, axis=0, keepdims=True))
    total = jnp.sum(factors * sums, axis=0)
    a3s[...] = (jnp.sum(factors * arrived[:, :, :lat], axis=0) / total).astype(bf16)
    start(c_a3, strips)

    each(1, pairs, lambda k: c_e3(k).wait_recv())
    summed = e3s[...].astype(f32)
    for k in range(1, pairs):
        summed = summed + e3r[k].astype(f32)
    e5[spot] = summed.astype(bf16)
    start(c_e5, spot_order)

    each(0, ny, lambda k: c_a3(k).wait_recv())
    finished = a3r[...].astype(f32).reshape((ny * 2 * per, lat)).astype(bf16)
    attn_o[...] = dot(attn_pick, finished).astype(bf16)

    each(1, nd, lambda k: c_e0(k).wait_send())
    each(1, corners, lambda k: c_t1(k).wait_send())
    each(1, corners, lambda k: c_a1(k).wait_send())
    each(1, pairs, lambda k: c_a2(k).wait_send())
    each(0, ny, lambda k: c_a3(k).wait_send())
    each(0, ny, lambda k: c_e1(k).wait_send())
    each(1, spots, lambda k: c_e2(k).wait_send())
    each(1, pairs, lambda k: c_e3(k).wait_send())

    each(1, spots, lambda k: c_e5(k).wait_recv())
    for k in range(spots):
        low, high = k * block, min((k + 1) * block, width)
        if low < width:
            mix_o[:, low:high] = dot(mix_pick, e5[k]).astype(bf16)
    each(1, spots, lambda k: c_e5(k).wait_send())


def placed_kernel(attention, mix, attn_o, mix_o):
    ny, hl = attn_o.shape[2], attn_o.shape[4]
    attended, mixed = attention[...].astype(f32), mix[...].astype(f32)
    for g in range(ny):
        mix_o[0, 0, g] = mixed[2 * g:2 * g + 2].astype(bf16)
        for j in range(2):
            low = (2 * g + j) * hl
            attn_o[0, 0, g, j] = attended[low:low + hl].astype(bf16)


def shards(
    cache_values, cache_rope, cache_scales, queries, new_keys, hidden_rows,
    expert_ids, expert_gates, owners, lengths, up_weight, down_weight,
):
    ny = lax.axis_size("dp")
    nd = ny * lax.axis_size("segment")
    nx = x_chips
    nz = lax.axis_size("ep") // nx
    cv, cr, cs, q = cache_values[0, 0], cache_rope[0, 0], cache_scales[0, 0], queries[0, 0]
    nk, xr, ids, gates = new_keys[0, 0], hidden_rows[0, 0], expert_ids[0, 0], expert_gates[0, 0]
    ctx, lat = cv.shape[1:]
    cols = q.shape[2]
    heads = cols // 2
    hl = heads // (nz * nx)
    width = up_weight.shape[1]
    corners, pairs = nx * 2, nz // 2
    spots = ny * corners
    block = -(-width // (spots * 128)) * 128
    sec = ny * 4
    rows_x = pairs * 4 * hl
    vmem = pl.BlockSpec(memory_space=pltpu.VMEM)
    anywhere = pl.BlockSpec(memory_space=pl.ANY)
    sems = lambda n: pltpu.SemaphoreType.DMA((n,))
    attention, mix = pl.pallas_call(
        functools.partial(kernel, (nd, ny, nz, nx)),
        out_shape=(
            jax.ShapeDtypeStruct((ny * 2 * hl, lat), bf16),
            jax.ShapeDtypeStruct((ny * 2, width), bf16),
        ),
        in_specs=[anywhere] * 12,
        out_specs=(vmem, vmem),
        scratch_shapes=[
            pltpu.VMEM(cv.shape, bf16),
            pltpu.VMEM(q.shape, bf16),
            pltpu.VMEM(up_weight.shape, bf16),
            pltpu.VMEM(down_weight.shape[:2] + (spots * block,), bf16),
            pltpu.VMEM(cr.shape, bf16),
            pltpu.VMEM(cs.shape, bf16),
            pltpu.VMEM(nk.shape, bf16),
            pltpu.VMEM(xr.shape, bf16),
            pltpu.VMEM(ids.shape, jnp.int32),
            pltpu.VMEM(gates.shape, bf16),
            pltpu.SMEM(owners[0, 0].shape, jnp.int32),
            pltpu.SMEM(lengths[0, 0].shape, jnp.int32),
            pltpu.VMEM((128, 128), f32),
            pltpu.VMEM((32, nk.shape[2]), f32),
            pltpu.VMEM((16, width // 4 + 128), f32),
            pltpu.VMEM((nd, 16, width // 4 + 128), bf16),
            pltpu.VMEM((corners, rows_x, lat), bf16),
            pltpu.VMEM((corners, rows_x, lat), bf16),
            pltpu.VMEM((corners, 8, 128), f32),
            pltpu.VMEM((corners, 8, 128), f32),
            pltpu.VMEM((pairs, 4 * hl, lat + 128), bf16),
            pltpu.VMEM((pairs, 4 * hl, lat + 128), bf16),
            pltpu.VMEM((4 * hl, lat), bf16),
            pltpu.VMEM((ny, 4 * hl, lat), bf16),
            pltpu.VMEM((ny, sec, corners * block), bf16),
            pltpu.VMEM((ny, sec, corners * block), bf16),
            pltpu.VMEM((ny, corners, sec, block), bf16),
            pltpu.VMEM((spots, sec, block), bf16),
            pltpu.VMEM((sec, block), bf16),
            pltpu.VMEM((pairs, sec, block), bf16),
            pltpu.VMEM((spots, sec, block), bf16),
            sems(12),
            sems(nd), sems(nd), sems(corners), sems(corners), sems(corners), sems(corners),
            sems(pairs), sems(pairs), sems(ny), sems(ny),
            sems(ny), sems(ny), sems(spots), sems(spots), sems(pairs), sems(pairs), sems(spots), sems(spots),
        ],
        compiler_params=pltpu.CompilerParams(
            collective_id=0, has_side_effects=True, vmem_limit_bytes=60 * 1024 * 1024
        ),
    )(cv, q, up_weight, down_weight, cr, cs, nk, xr, ids, gates, owners[0, 0], lengths[0, 0])
    return pl.pallas_call(
        placed_kernel,
        out_shape=(
            jax.ShapeDtypeStruct((1, 1, ny, 2, hl, lat), bf16),
            jax.ShapeDtypeStruct((1, 1, ny, 2, width), bf16),
        ),
        in_specs=[vmem] * 2,
        out_specs=(vmem, vmem),
    )(attention, mix)


def solution(mesh):
    placed = (
        P("segment", "dp", None, "ep", None),
        P("segment", "dp", None, None, "ep"),
        P("segment", "dp", None, None, "ep"),
        P("segment", "dp", None, None, None),
        P("segment", "dp", None, None, None),
        P("segment", "dp", None, None, None),
        P("segment", "dp", None, None, None),
        P("segment", "dp", None, None, None),
        P("segment", "dp", None),
        P("segment", "dp", None),
        P("ep", None, ("segment", "dp")),
        P("ep", ("segment", "dp"), None),
    )
    return jax.shard_map(
        shards,
        mesh=mesh,
        in_specs=placed,
        out_specs=(
            P("segment", "dp", None, None, "ep", None),
            P("segment", "dp", None, None, None),
        ),
        check_vma=False,
    )
```

```python
import functools

import jax
import jax.numpy as jnp
from jax import lax
from jax.experimental import pallas as pl
from jax.experimental.pallas import tpu as pltpu
from jax.sharding import PartitionSpec as P

score_scale = 192.0 ** (-0.5)
far_below = -1e30
x_chips = 4
MESH = pl.DeviceIdType.MESH
f32 = jnp.float32
bf16 = jnp.bfloat16


def iota(shape, dim):
    return lax.broadcasted_iota(jnp.int32, shape, dim)


def dot(a, b):
    return jnp.dot(a, b, preferred_element_type=f32)


def dot_rows(a, b):
    return lax.dot_general(a, b, (((1,), (1,)), ((), ())), preferred_element_type=f32)


def dot_cols(a, b):
    return lax.dot_general(a, b, (((0,), (0,)), ((), ())), preferred_element_type=f32)


def three_parts(value):
    high = value.astype(bf16).astype(f32)
    rest = value - high
    middle = rest.astype(bf16).astype(f32)
    low = (rest - middle).astype(bf16).astype(f32)
    return high, middle, low


def kernel(
    sizes,
    cv_h, q_h, up_h, dn_h, cr_h, cs_h, nk_h, xr_h, ids_h, gates_h, owners_h, lengths_h,
    attn_o, mix_o,
    cv, q, up, dn, cr, cs, nk, xr, ids, gates, owners, lengths, tr, nkp, xf, xg,
    a1s, a1r, t1s, t1r, a2s, a2r, a3s, a3r,
    e1s, e1r, e2s, e2r, e3s, e3r, e5,
    in_sem, line_in,
    e0_ss, e0_rs, a1_ss, a1_rs, t1_ss, t1_rs, a2_ss, a2_rs, a3_ss, a3_rs,
    e1_ss, e1_rs, e2_ss, e2_rs, e3_ss, e3_rs, e5_ss, e5_rs,
):
    nd, ny, nz, nx = sizes
    s, y, ep = lax.axis_index("segment"), lax.axis_index("dp"), lax.axis_index("ep")
    z, x = ep // nx, lax.rem(ep, nx)
    d = s * ny + y
    ctx, lat = cv.shape[1], cv.shape[2]
    cols = q.shape[2]
    heads = cols // 2
    hl = heads // (nz * nx)
    width = up.shape[1]
    quarter = width // 4
    pair, side, pairs = z // 2, lax.rem(z, 2), nz // 2
    corner = x * 2 + side
    corners = nx * 2
    spot = y * corners + corner
    spots = ny * corners
    block = e2s.shape[3]
    strip = corners * block
    rows_x = a1s.shape[1]
    sec = ny * 4

    def plane(k):
        to = lax.rem(d + k, nd)
        return to, {"segment": to // ny, "dp": lax.rem(to, ny)}

    def near(k):
        to_x = lax.rem(x + k // 2, nx)
        to_side = lax.rem(side + k % 2, 2)
        return to_x * 2 + to_side, {"ep": (pair * 2 + to_side) * nx + to_x}

    def both_planes(k):
        to_y = lax.rem(y + k // corners, ny)
        to_x = lax.rem(x + (k // 2) % nx, nx)
        to_side = lax.rem(side + k % 2, 2)
        return (to_y * nx + to_x) * 2 + to_side, {
            "dp": to_y, "ep": (pair * 2 + to_side) * nx + to_x,
        }

    def far(k):
        to = lax.rem(pair + k, pairs)
        return to, {"ep": (to * 2 + side) * nx + x}

    def across(k):
        to = lax.rem(y + k, ny)
        return to, {"segment": 1 - s, "dp": to}

    def remote(src, dst, ss, rs, k, to):
        return pltpu.make_async_remote_copy(
            src_ref=src, dst_ref=dst, send_sem=ss.at[k], recv_sem=rs.at[k],
            device_id=to, device_id_type=MESH,
        )

    def c_e0(k):
        return remote(xg.at[d], xg.at[d], e0_ss, e0_rs, k, plane(k)[1])

    def c_a1(k):
        to, dev = near(k)
        return remote(a1s.at[to], a1r.at[k], a1_ss, a1_rs, k, dev)

    def c_t1(k):
        to, dev = near(k)
        return remote(t1s.at[to], t1r.at[k], t1_ss, t1_rs, k, dev)

    def c_a2(k):
        to, dev = far(k)
        return remote(a2s.at[to], a2r.at[k], a2_ss, a2_rs, k, dev)

    def c_a3(k):
        return remote(a3s, a3r.at[y], a3_ss, a3_rs, k, across(k)[1])

    def c_e1(k):
        return remote(e1s.at[k], e1r.at[k], e1_ss, e1_rs, k, {"segment": 1 - s})

    def c_e2(k):
        to, dev = both_planes(k)
        return remote(e2s.at[k // corners, lax.rem(to, corners)], e2r.at[k], e2_ss, e2_rs, k, dev)

    def c_e3(k):
        return remote(e3s, e3r.at[k], e3_ss, e3_rs, k, far(k)[1])

    def c_e5(k):
        return remote(e5.at[spot], e5.at[spot], e5_ss, e5_rs, k, both_planes(k)[1])

    def each(first, last, act):
        for k in range(first, last):
            act(k)

    def ring(k, n):
        return min(k % n, -k % n)

    def farthest(first, last, hops):
        return sorted(range(first, last), key=lambda k: -hops(k))

    plane_order = farthest(1, nd, lambda k: ring(k, ny) if k % ny else 0.5)
    near_order = farthest(1, corners, lambda k: ring(k // 2, nx) + k % 2)
    far_order = farthest(1, pairs, lambda k: ring(k, pairs))
    strips = farthest(0, ny, lambda k: ring(k, ny))
    corner_order = farthest(0, corners, lambda k: ring(k // 2, nx) + k % 2)
    spot_order = farthest(
        1, spots, lambda k: ring(k // corners, ny) + ring((k % corners) // 2, nx) + k % 2
    )

    def start(copy, order):
        for k in order:
            copy(k).start()

    barrier = pltpu.get_barrier_semaphore()

    def greet(where):
        def act(k):
            pl.semaphore_signal(barrier, inc=1, device_id=where(k)[1], device_id_type=MESH)

        return act

    for k in far_order:
        greet(far)(k)
    for k in near_order:
        greet(near)(k)
    for k in plane_order:
        greet(plane)(k)

    loads = {}
    for n, (name, src, dst) in enumerate((
        ("rows", xr_h, xr), ("ids", ids_h, ids), ("gates", gates_h, gates), ("owners", owners_h, owners),
        ("values", cv_h, cv), ("scales", cs_h, cs), ("queries", q_h, q), ("rope", cr_h, cr),
        ("fresh", nk_h, nk), ("lengths", lengths_h, lengths), ("up", up_h, up), ("down", dn_h, dn.at[:, :, :width]),
    )):
        loads[name] = pltpu.make_async_copy(src, dst, in_sem.at[n])
        loads[name].start()

    xf[...] = jnp.zeros_like(xf)
    for name in ("rows", "ids", "gates", "owners"):
        loads[name].wait()
    for r in range(2):
        for j in range(2):
            i = 2 * r + j
            row = xr[r, j:j + 1, :].astype(f32)
            for part in range(4):
                xf[4 * i + part:4 * i + part + 1, :quarter] = row[:, part * quarter:(part + 1) * quarter]
            xf[4 * i:4 * i + 1, quarter:quarter + 8] = ids[r, j:j + 1, :].astype(f32)
            xf[4 * i + 1:4 * i + 2, quarter:quarter + 8] = gates[r, j:j + 1, :].astype(f32)
            xf[4 * i + 2:4 * i + 3, quarter:] = jnp.full((1, 128), owners[r], jnp.int32).astype(f32)
    xg[d] = xf[...].astype(bf16)

    tr[...] = jnp.zeros_like(tr)
    nkp[...] = jnp.zeros_like(nkp)
    loads["scales"].wait()
    loads["fresh"].wait()
    for r in range(2):
        tr[8 * r:8 * r + 4, :ctx] = cs[r].astype(f32)
        nkp[16 * r:16 * r + 2, :] = nk[r].astype(f32)
    scale_cols = tr[:, :ctx].T
    total_rows = corners * rows_x
    per = 2 * hl
    place = iota((total_rows, heads), 0)
    shift = lambda n: n.bit_length() - 1
    h_of = place & (hl - 1)
    j_of = (place >> shift(hl)) & 1
    r_of = (place >> shift(per)) & 1
    pair_of = (place >> shift(2 * per)) & (pairs - 1)
    side_of = (place >> shift(2 * per * pairs)) & 1
    x_of = place >> shift(4 * per * pairs)
    head_of = ((pair_of * 2 + side_of) * nx + x_of) * hl + h_of
    match = head_of == iota((total_rows, heads), 1)
    orders = [
        jnp.concatenate(
            [jnp.where(match & (r_of == r) & (j_of == j), 1.0, 0.0).astype(bf16) for j in range(2)],
            axis=1,
        )
        for r in range(2)
    ]
    for name in ("values", "queries", "rope", "lengths"):
        loads[name].wait()
    out = jnp.zeros((total_rows, lat), f32)
    stats = jnp.zeros((16, total_rows), f32)
    for r in range(2):
        latent = jnp.concatenate(
            [
                cv[r, :, b * 128:(b + 1) * 128].astype(f32) * scale_cols[:, 8 * r + b:8 * r + b + 1]
                for b in range(lat // 128)
            ],
            axis=1,
        ).astype(bf16)
        fresh = nkp[16 * r:16 * r + 16, :].astype(bf16)
        cached = dot(latent, q[r, :lat, :]) + dot_cols(cr[r], q[r, lat:, :])
        newer = dot(fresh[:, :lat], q[r, :lat, :]) + dot(fresh[:, lat:], q[r, lat:, :])
        cached_ok = ep * ctx + iota((ctx, cols), 0) < lengths[r]
        newer_ok = (iota((16, cols), 0) + jnp.where(ep == 0, 0, 16)) <= (iota((16, cols), 1) // heads)
        cached = jnp.where(cached_ok, cached * score_scale, far_below)
        newer = jnp.where(newer_ok, newer * score_scale, far_below)
        peak = jnp.maximum(
            jnp.max(cached, axis=0, keepdims=True), jnp.max(newer, axis=0, keepdims=True)
        )
        cached = jnp.where(cached_ok, jnp.exp(cached - peak), 0.0)
        newer = jnp.where(newer_ok, jnp.exp(newer - peak), 0.0)
        total = jnp.sum(cached, axis=0, keepdims=True) + jnp.sum(newer, axis=0, keepdims=True)
        line = iota((16, cols), 0)
        extra = jnp.zeros((16, cols), f32)
        for n, part in enumerate(three_parts(peak) + three_parts(total)):
            extra = jnp.where(line == n, part, extra)
        order = orders[r]
        out = out + dot(dot_rows(order, cached.astype(bf16)).astype(bf16), latent)
        out = out + dot(dot_rows(order, newer.astype(bf16)).astype(bf16), fresh[:, :lat])
        stats = stats + dot_rows(extra.astype(bf16), order)
    t1s[...] = jnp.zeros_like(t1s)
    peak = stats[0:1] + stats[1:2] + stats[2:3]
    total = stats[3:4] + stats[4:5] + stats[5:6]
    for to in range(corners):
        a1s[to] = out[to * rows_x:(to + 1) * rows_x].astype(bf16)
        t1s[to, 0:1, :rows_x] = peak[:, to * rows_x:(to + 1) * rows_x]
        t1s[to, 1:2, :rows_x] = total[:, to * rows_x:(to + 1) * rows_x]
    pl.semaphore_wait(barrier, (pairs - 1) + (nd - 1) + (corners - 1))
    start(c_e0, plane_order)
    for k in near_order:
        pl.semaphore_signal(line_in, inc=1, device_id=near(k)[1], device_id_type=MESH)
    start(c_t1, near_order)
    start(c_a1, near_order)

    row_count = nd * 4
    want = iota((3 * row_count, nd * 16), 0)
    pick = iota((3 * row_count, nd * 16), 1) == 4 * lax.rem(want, row_count) + want // row_count
    pick = jnp.where(pick, 1.0, 0.0).astype(bf16)
    lane = iota((row_count, 128), 1)
    experts, hidden_width = up.shape[0], up.shape[2]
    if dn.shape[2] > width:
        dn[:, :, width:] = jnp.zeros((experts, hidden_width, dn.shape[2] - width), bf16)
    part_of = lax.rem(iota((nd * 16, experts * hidden_width), 0), 4)
    loads["up"].wait()
    loads["down"].wait()
    each(1, nd, lambda k: c_e0(k).wait_recv())
    gathered = xg[...].reshape((nd * 16, xg.shape[2]))
    acc = jnp.zeros((nd * 16, experts * hidden_width), f32)
    for part in range(4):
        weights = jnp.concatenate(
            [up[e, part * quarter:(part + 1) * quarter, :] for e in range(experts)], axis=1
        )
        acc = jnp.where(part_of == part, dot(gathered[:, :quarter], weights), acc)
    notes = gathered[:, quarter:]
    routing = dot(pick, notes)
    chosen, gate_values = routing[:row_count], routing[row_count:2 * row_count]
    acc = acc + pltpu.roll(acc, nd * 16 - 1, 0)
    acc = acc + pltpu.roll(acc, nd * 16 - 2, 0)
    hidden = (acc / (1.0 + jnp.exp(-acc))).astype(bf16)
    hidden = dot(pick[:row_count], hidden).astype(bf16)
    hiddens, expert_gates = [], []
    for e in range(experts):
        expert = (ep * experts + e).astype(f32)
        expert_gates.append(jnp.sum(
            jnp.where((chosen == expert) & (lane < 8), gate_values, 0.0), axis=1, keepdims=True
        ))
        hiddens.append(hidden[:, e * hidden_width:(e + 1) * hidden_width])
    owns = {}
    for j in strips:
        low = pl.multiple_of(lax.rem(y + j, ny) * strip, 128)
        partial = jnp.zeros((row_count, strip), f32)
        for e in range(experts):
            partial = partial + expert_gates[e] * dot(hiddens[e], dn[e, :, pl.ds(low, strip)])
        first, second = partial[:sec], partial[sec:]
        e1s[j] = jnp.where(s == 0, first, second).astype(bf16)
        c_e1(j).start()
        owns[j] = jnp.where(s == 0, second, first)

    pl.semaphore_wait(line_in, corners - 1)
    for j in strips:
        c_e1(j).wait_recv()
        own = owns[j] + e1r[j].astype(f32)
        for to in range(corners):
            e2s[j, to] = own[:, to * block:(to + 1) * block].astype(bf16)
        start(c_e2, [k for k in (j * corners + c for c in corner_order) if k])

    each(1, corners, lambda k: c_t1(k).wait_recv())
    tops = [t1s[corner, 0:1, :rows_x]] + [t1r[k, 0:1, :rows_x] for k in range(1, corners)]
    sums = [t1s[corner, 1:2, :rows_x]] + [t1r[k, 1:2, :rows_x] for k in range(1, corners)]
    top = functools.reduce(jnp.maximum, tops)
    factors = [jnp.exp(one - top) for one in tops]
    total = functools.reduce(jnp.add, [a * b for a, b in zip(factors, sums)])
    tr[...] = jnp.zeros_like(tr)
    for n, one in enumerate(list(three_parts(top) + three_parts(total)) + factors):
        tr[n:n + 1, :rows_x] = one
    turned = tr[...].T[:rows_x]
    each(1, corners, lambda k: c_a1(k).wait_recv())
    merged = turned[:, 6:7] * a1s[corner].astype(f32)
    for k in range(1, corners):
        merged = merged + turned[:, 6 + k:7 + k] * a1r[k].astype(f32)
    a2s[:, :, :lat] = merged.reshape((pairs, 2 * per, lat)).astype(bf16)
    a2s[:, :, lat:] = turned.reshape((pairs, 2 * per, 128)).astype(bf16)
    start(c_a2, far_order)

    each(1, spots, lambda k: c_e2(k).wait_recv())
    summed = e2s[0, corner].astype(f32)
    for k in range(1, spots):
        summed = summed + e2r[k].astype(f32)
    e3s[...] = summed.astype(bf16)
    start(c_e3, far_order)

    first_row = jnp.where(s == 0, ny * 16, 0)
    owner_lane = jnp.where(iota((16, 128), 1) == 0, 1.0, 0.0).astype(bf16)

    def owner_row(count, split):
        row = iota((count, nd * 16), 0)
        source = first_row + 4 * (row // split) + 2
        pull = jnp.where(iota((count, nd * 16), 1) == source, 1.0, 0.0).astype(bf16)
        return dot_rows(owner_lane, dot(pull, notes).astype(bf16))[0:1]

    mine = y.astype(f32)
    out_i, in_i = iota((2 * ny, sec), 0), iota((2 * ny, sec), 1)
    mix_pick = (out_i // 2 == in_i // 4) & (lax.rem(out_i, 2) == lax.rem(in_i, 2))
    mix_pick = jnp.where(mix_pick & (owner_row(sec, 1) == mine), 1.0, 0.0).astype(bf16)
    out_i, in_i = iota((2 * per // 2 * ny, 2 * per * ny), 0), iota((2 * per // 2 * ny, 2 * per * ny), 1)
    attn_pick = (out_i // per == in_i // (2 * per)) & (lax.rem(out_i, per) == lax.rem(in_i, per))
    attn_pick = jnp.where(attn_pick & (owner_row(2 * per * ny, hl) == mine), 1.0, 0.0).astype(bf16)

    a2r[0] = a2s[pair]
    each(1, pairs, lambda k: c_a2(k).wait_recv())
    arrived = a2r[...].astype(f32)
    tops = arrived[:, :, lat:lat + 1] + arrived[:, :, lat + 1:lat + 2] + arrived[:, :, lat + 2:lat + 3]
    sums = arrived[:, :, lat + 3:lat + 4] + arrived[:, :, lat + 4:lat + 5] + arrived[:, :, lat + 5:lat + 6]
    factors = jnp.exp(tops - jnp.max(tops, axis=0, keepdims=True))
    total = jnp.sum(factors * sums, axis=0)
    a3s[...] = (jnp.sum(factors * arrived[:, :, :lat], axis=0) / total).astype(bf16)
    start(c_a3, strips)

    each(1, pairs, lambda k: c_e3(k).wait_recv())
    summed = e3s[...].astype(f32)
    for k in range(1, pairs):
        summed = summed + e3r[k].astype(f32)
    e5[spot] = summed.astype(bf16)
    start(c_e5, spot_order)

    each(0, ny, lambda k: c_a3(k).wait_recv())
    finished = a3r[...].astype(f32).reshape((ny * 2 * per, lat)).astype(bf16)
    attn_o[...] = dot(attn_pick, finished).astype(bf16)

    each(1, nd, lambda k: c_e0(k).wait_send())
    each(1, corners, lambda k: c_t1(k).wait_send())
    each(1, corners, lambda k: c_a1(k).wait_send())
    each(1, pairs, lambda k: c_a2(k).wait_send())
    each(0, ny, lambda k: c_a3(k).wait_send())
    each(0, ny, lambda k: c_e1(k).wait_send())
    each(1, spots, lambda k: c_e2(k).wait_send())
    each(1, pairs, lambda k: c_e3(k).wait_send())

    each(1, spots, lambda k: c_e5(k).wait_recv())
    for k in range(spots):
        low, high = k * block, min((k + 1) * block, width)
        if low < width:
            mix_o[:, low:high] = dot(mix_pick, e5[k]).astype(bf16)
    each(1, spots, lambda k: c_e5(k).wait_send())


def placed_kernel(attention, mix, attn_o, mix_o):
    ny, hl = attn_o.shape[2], attn_o.shape[4]
    attended, mixed = attention[...].astype(f32), mix[...].astype(f32)
    for g in range(ny):
        mix_o[0, 0, g] = mixed[2 * g:2 * g + 2].astype(bf16)
        for j in range(2):
            low = (2 * g + j) * hl
            attn_o[0, 0, g, j] = attended[low:low + hl].astype(bf16)


def shards(
    cache_values, cache_rope, cache_scales, queries, new_keys, hidden_rows,
    expert_ids, expert_gates, owners, lengths, up_weight, down_weight,
):
    ny = lax.axis_size("dp")
    nd = ny * lax.axis_size("segment")
    nx = x_chips
    nz = lax.axis_size("ep") // nx
    cv, cr, cs, q = cache_values[0, 0], cache_rope[0, 0], cache_scales[0, 0], queries[0, 0]
    nk, xr, ids, gates = new_keys[0, 0], hidden_rows[0, 0], expert_ids[0, 0], expert_gates[0, 0]
    ctx, lat = cv.shape[1:]
    cols = q.shape[2]
    heads = cols // 2
    hl = heads // (nz * nx)
    width = up_weight.shape[1]
    corners, pairs = nx * 2, nz // 2
    spots = ny * corners
    block = -(-width // (spots * 128)) * 128
    sec = ny * 4
    rows_x = pairs * 4 * hl
    vmem = pl.BlockSpec(memory_space=pltpu.VMEM)
    anywhere = pl.BlockSpec(memory_space=pl.ANY)
    sems = lambda n: pltpu.SemaphoreType.DMA((n,))
    attention, mix = pl.pallas_call(
        functools.partial(kernel, (nd, ny, nz, nx)),
        out_shape=(
            jax.ShapeDtypeStruct((ny * 2 * hl, lat), bf16),
            jax.ShapeDtypeStruct((ny * 2, width), bf16),
        ),
        in_specs=[anywhere] * 12,
        out_specs=(vmem, vmem),
        scratch_shapes=[
            pltpu.VMEM(cv.shape, bf16),
            pltpu.VMEM(q.shape, bf16),
            pltpu.VMEM(up_weight.shape, bf16),
            pltpu.VMEM(down_weight.shape[:2] + (spots * block,), bf16),
            pltpu.VMEM(cr.shape, bf16),
            pltpu.VMEM(cs.shape, bf16),
            pltpu.VMEM(nk.shape, bf16),
            pltpu.VMEM(xr.shape, bf16),
            pltpu.VMEM(ids.shape, jnp.int32),
            pltpu.VMEM(gates.shape, bf16),
            pltpu.SMEM(owners[0, 0].shape, jnp.int32),
            pltpu.SMEM(lengths[0, 0].shape, jnp.int32),
            pltpu.VMEM((128, 128), f32),
            pltpu.VMEM((32, nk.shape[2]), f32),
            pltpu.VMEM((16, width // 4 + 128), f32),
            pltpu.VMEM((nd, 16, width // 4 + 128), bf16),
            pltpu.VMEM((corners, rows_x, lat), bf16),
            pltpu.VMEM((corners, rows_x, lat), bf16),
            pltpu.VMEM((corners, 8, 128), f32),
            pltpu.VMEM((corners, 8, 128), f32),
            pltpu.VMEM((pairs, 4 * hl, lat + 128), bf16),
            pltpu.VMEM((pairs, 4 * hl, lat + 128), bf16),
            pltpu.VMEM((4 * hl, lat), bf16),
            pltpu.VMEM((ny, 4 * hl, lat), bf16),
            pltpu.VMEM((ny, sec, corners * block), bf16),
            pltpu.VMEM((ny, sec, corners * block), bf16),
            pltpu.VMEM((ny, corners, sec, block), bf16),
            pltpu.VMEM((spots, sec, block), bf16),
            pltpu.VMEM((sec, block), bf16),
            pltpu.VMEM((pairs, sec, block), bf16),
            pltpu.VMEM((spots, sec, block), bf16),
            sems(12), pltpu.SemaphoreType.REGULAR,
            sems(nd), sems(nd), sems(corners), sems(corners), sems(corners), sems(corners),
            sems(pairs), sems(pairs), sems(ny), sems(ny),
            sems(ny), sems(ny), sems(spots), sems(spots), sems(pairs), sems(pairs), sems(spots), sems(spots),
        ],
        compiler_params=pltpu.CompilerParams(
            collective_id=0, has_side_effects=True, vmem_limit_bytes=60 * 1024 * 1024
        ),
    )(cv, q, up_weight, down_weight, cr, cs, nk, xr, ids, gates, owners[0, 0], lengths[0, 0])
    return pl.pallas_call(
        placed_kernel,
        out_shape=(
            jax.ShapeDtypeStruct((1, 1, ny, 2, hl, lat), bf16),
            jax.ShapeDtypeStruct((1, 1, ny, 2, width), bf16),
        ),
        in_specs=[vmem] * 2,
        out_specs=(vmem, vmem),
    )(attention, mix)


def solution(mesh):
    placed = (
        P("segment", "dp", None, "ep", None),
        P("segment", "dp", None, None, "ep"),
        P("segment", "dp", None, None, "ep"),
        P("segment", "dp", None, None, None),
        P("segment", "dp", None, None, None),
        P("segment", "dp", None, None, None),
        P("segment", "dp", None, None, None),
        P("segment", "dp", None, None, None),
        P("segment", "dp", None),
        P("segment", "dp", None),
        P("ep", None, ("segment", "dp")),
        P("ep", ("segment", "dp"), None),
    )
    return jax.shard_map(
        shards,
        mesh=mesh,
        in_specs=placed,
        out_specs=(
            P("segment", "dp", None, None, "ep", None),
            P("segment", "dp", None, None, None),
        ),
        check_vma=False,
    )
```
